32 devices in a mesh: grp: 2 (over y), aux: 16 (over z, x, core).
Axes of the slice: x: 2, y: 2, z: 4, core: 2. Of those that a mesh axis runs over, the one named last changes fastest.
Arguments:
- rhs: float32 [512, 2, 1024], P(('grp', 'aux')), parts along dimension 0, may hold values from -6 to 6
- occ_energy: float32 [512], P('grp'), parts along dimension 0, may hold values from -1.5 to -0.3
- vir_energy: float32 [2048], P('grp'), parts along dimension 0, may hold values from 0.2 to 3
- occ_ints: bfloat16 [128, 256, 256], P(('grp', 'aux')), parts along dimension 0, may hold values from -0.046875 to 0.046875
- vir_ints: bfloat16 [128, 1024, 1024], P(('grp', 'aux')), parts along dimension 0, may hold values from -0.1875 to 0.1875
Outputs:
- response: float32 [512, 2, 1024], P(('grp', 'aux')), parts along dimension 0
The draws below stay inside these ranges and needn't reach their ends.
There are 2 independent parts, one for each index of `grp`. The reference program is written for one: setup_inputs(seed, part) draws one part's arguments, and reference() takes and returns one part's arrays. A program takes and returns all parts, laid end to end along the dimension named above; each array names one. Nothing has to cross between parts.
All inputs are finite; a program needn't handle non-finite values.
Results may differ from the reference program's by a relative error of at most 0.0015.
Values may be sent and summed in bfloat16 or wider, within the bound.
A program may use at most 64 MiB of HBM per device.

```python
import jax
import jax.numpy as jnp
from jax import lax

NOCC = 256
NVIR = 1024
NSTATE = 2
ITERS = 2
NAUX = 64


def strengthened(entries, own_key, source, target, shards_of, factor):
    def block_of(axis_at):
        return (jnp.arange(entries.shape[axis_at]) // (entries.shape[axis_at] // shards_of)).reshape((-1,) + (1,) * (entries.ndim - 1 - axis_at))

    one_side = jax.random.permutation(own_key, shards_of)[block_of(target)]
    far = (block_of(target) + shards_of // 2) % shards_of
    return jnp.where((block_of(source) == one_side) | (block_of(source) == far), factor * entries, entries)


def shard_levels(own_key, extent, shards, least, top_value):
    level = 1.0
    for axis_at, parts in shards:
        draws = jax.random.uniform(jax.random.fold_in(jax.random.fold_in(own_key, 6), axis_at), (parts,), jnp.float32, least / len(shards), top_value / len(shards))
        level = level * jnp.repeat(jnp.exp(draws), extent[axis_at] // parts).reshape((-1,) + (1,) * (len(extent) - 1 - axis_at))
    return level


def noise(key, extent, spread, most, split=(), dtype=jnp.bfloat16):
    gain = shard_levels(key, extent, split, -0.22, 0.18) if split else 1.0
    drawn = jax.random.normal(key, extent, jnp.float32) * spread * gain
    return jnp.minimum(jnp.maximum(drawn, -most), most).astype(dtype)


def gaussian_with(own_key, dims, scale, reach, split, heavy, dtype=jnp.bfloat16):
    result = scale * jax.random.normal(own_key, dims, jnp.float32)
    if split:
        result = result * shard_levels(own_key, dims, split, -0.22, 0.18)
    return jnp.clip(strengthened(result, jax.random.fold_in(own_key, 3), *heavy), -reach, reach).astype(dtype)


def setup_inputs(seed: int = 0, part: int = 0) -> dict:
    arg_keys = jax.random.split(jax.random.key(seed), 6)
    part_splits = jax.random.split(jax.random.fold_in(arg_keys[5], part), 6)
    rhs = noise(part_splits[0], (NOCC, NSTATE, NVIR), 1.0, 6.0, ((0, 16),), jnp.float32)
    occ_energy = jnp.clip(jax.random.uniform(part_splits[1], (NOCC,), jnp.float32, -1.5, -0.3), -1.5, -0.3)
    vir_energy = jnp.clip(jax.random.uniform(part_splits[2], (NVIR,), jnp.float32, 0.2, 3.0), 0.2, 3.0)
    occ_ints = gaussian_with(part_splits[3], (NAUX, NOCC, NOCC), (2 * NOCC * NAUX) ** -0.5, 0.046875, ((0, 16),), (0, 1, 16, 2.0))
    vir_ints = noise(part_splits[4], (NAUX, NVIR, NVIR), NVIR ** -0.5, 0.1875, ((0, 16),))
    return {"rhs": rhs, "occ_energy": occ_energy, "vir_energy": vir_energy, "occ_ints": occ_ints, "vir_ints": vir_ints}


def reference(rhs, occ_energy, vir_energy, occ_ints, vir_ints):
    denom = vir_energy[None, None, :] - occ_energy[:, None, None]
    response = rhs / denom
    for step in range(ITERS):
        rounded = response.astype(jnp.bfloat16).reshape(NOCC, NSTATE * NVIR)

        def accumulate(total, pair):
            occ_block, vir_block = pair
            half = jnp.dot(occ_block, rounded, preferred_element_type=jnp.float32).astype(jnp.bfloat16)
            half = half.reshape(NOCC * NSTATE, NVIR)
            term = lax.dot_general(half, vir_block, (((1,), (1,)), ((), ())), preferred_element_type=jnp.float32)
            return total + term, None

        start = jnp.zeros((NOCC * NSTATE, NVIR), jnp.float32)
        exchange, unused = lax.scan(accumulate, start, (occ_ints, vir_ints))
        exchange = exchange.reshape(NOCC, NSTATE, NVIR)
        response = 0.4 * response + 0.6 * (rhs - exchange) / denom
    return response
```

```python
import functools

import jax
import jax.numpy as jnp
from jax import lax
from jax.experimental import pallas as pl
from jax.experimental.pallas import tpu as pltpu
from jax.sharding import PartitionSpec as P

ITERS = 2
CHUNKS = 2
MESH = pl.DeviceIdType.MESH
F32 = jnp.float32
BF16 = jnp.bfloat16


def kernel(
    nz, rhs, occ_e, vir_e, occ_hbm, vir_hbm, out,
    occ_v, vir_v, denom, resp, ag, half, ex, cr, xo, xs, xr, zo, zs, zr,
    load_sem, agz_s, agz_r, agx_s, agx_r, agc_s, agc_r,
    rc_s, rc_r, rx_s, rx_r, rz_s, rz_r,
):
    rows, states, nvir = rhs.shape
    nocc = half.shape[0]
    local_aux = occ_v.shape[0]
    width = nvir // CHUNKS
    grp = lax.axis_index("grp")
    me = lax.axis_index("aux")
    c = lax.rem(me, 2)
    x = lax.rem(me // 2, 2)
    z = me // 4

    def dev(zz, xx, cc):
        return (grp, (zz * 2 + xx) * 2 + cc)

    def up(k):
        return lax.rem(z + k, nz)

    def down(k):
        return lax.rem(z + nz - k, nz)

    sibling = dev(z, x, 1 - c)
    across = dev(z, 1 - x, c)

    loads = [pltpu.make_async_copy(occ_hbm, occ_v, load_sem.at[local_aux])]
    for p in range(local_aux):
        loads.append(
            pltpu.make_async_copy(vir_hbm.at[p], vir_v.at[:, pl.ds(p * nvir, nvir)], load_sem.at[p])
        )
    for load in loads:
        load.start()

    barrier = pltpu.get_barrier_semaphore()
    for peer in [sibling, across] + [dev(up(k), x, c) for k in range(1, nz)]:
        pl.semaphore_signal(barrier, inc=1, device_id=peer, device_id_type=MESH)

    picked = lax.broadcasted_iota(jnp.int32, (rows, nocc), 1) == (
        lax.broadcasted_iota(jnp.int32, (rows, nocc), 0) + me * rows
    )
    own_occ = jnp.sum(jnp.where(picked, occ_e[...], 0.0), axis=1, keepdims=True)
    denom[...] = vir_e[...] - own_occ
    for s in range(states):
        resp[s] = rhs[:, s, :] / denom[...]
    pl.semaphore_wait(barrier, nz + 1)

    sent = []

    def send(src, dst, s_sem, r_sem, to):
        copy = pltpu.make_async_remote_copy(
            src_ref=src, dst_ref=dst, send_sem=s_sem, recv_sem=r_sem, device_id=to, device_id_type=MESH
        )
        copy.start()
        sent.append(copy)

    def arrived(dst, s_sem, r_sem, frm):
        pltpu.make_async_remote_copy(
            src_ref=dst, dst_ref=dst, send_sem=s_sem, recv_sem=r_sem, device_id=frm, device_id_type=MESH
        ).wait_recv()

    near_first = sorted(range(1, nz), key=lambda k: min(k, nz - k))

    def ag_start(it, s):
        block = ag.at[it, s, z, x, c]
        block[...] = resp[s].astype(BF16)
        for k in near_first:
            send(block, block, agz_s.at[it, s, k], agz_r.at[it, s, k], dev(up(k), x, c))
        send(block, block, agx_s.at[it, s, 0], agx_r.at[it, s, 0], across)

    def ag_z(it, s):
        for k in near_first:
            block = ag.at[it, s, down(k), x, c]
            arrived(block, agz_s.at[it, s, k], agz_r.at[it, s, k], dev(down(k), x, c))
            send(block, block, agx_s.at[it, s, k], agx_r.at[it, s, k], across)
        line = ag.at[it, s, :, x, c]
        send(line, line, agc_s.at[it, s, 0], agc_r.at[it, s, 0], sibling)

    def ag_x(it, s):
        for k in [0] + near_first:
            block = ag.at[it, s, down(k), 1 - x, c]
            arrived(block, agx_s.at[it, s, k], agx_r.at[it, s, k], across)
        line = ag.at[it, s, :, 1 - x, c]
        send(line, line, agc_s.at[it, s, 1], agc_r.at[it, s, 1], sibling)

    def ag_c(it, s):
        arrived(ag.at[it, s, :, x, 1 - c], agc_s.at[it, s, 0], agc_r.at[it, s, 0], sibling)
        arrived(ag.at[it, s, :, 1 - x, 1 - c], agc_s.at[it, s, 1], agc_r.at[it, s, 1], sibling)

    def halves(it, s):
        gathered = ag[it, s].reshape(nocc, nvir)
        for p in range(local_aux):
            product = jnp.dot(occ_v[p], gathered, preferred_element_type=F32)
            half[:, pl.ds(p * nvir, nvir)] = product.astype(BF16)

    def exchange(it, s, ch):
        cols = pl.ds(ch * width, width)
        product = lax.dot_general(
            half[...], vir_v[cols, :], (((1,), (1,)), ((), ())), preferred_element_type=F32
        )
        ex[it, s, :, :, :, :, cols] = product.reshape(nz, 2, 2, rows, width)
        send(
            ex.at[it, s, :, :, 1 - c, :, cols], cr.at[it, s, :, :, :, cols],
            rc_s.at[it, s, ch], rc_r.at[it, s, ch], sibling,
        )

    def rs_x(it, s, ch):
        cols = pl.ds(ch * width, width)
        arrived(cr.at[it, s, :, :, :, cols], rc_s.at[it, s, ch], rc_r.at[it, s, ch], sibling)
        xs[it, s, :, :, cols] = (
            ex[it, s, :, 1 - x, c, :, cols] + cr[it, s, :, 1 - x, :, cols]
        ).astype(BF16)
        send(
            xs.at[it, s, :, :, cols], xr.at[it, s, :, :, cols],
            rx_s.at[it, s, ch], rx_r.at[it, s, ch], across,
        )
        xo[s, :, :, cols] = ex[it, s, :, x, c, :, cols] + cr[it, s, :, x, :, cols]

    def rs_z(it, s, ch):
        cols = pl.ds(ch * width, width)
        arrived(xr.at[it, s, :, :, cols], rx_s.at[it, s, ch], rx_r.at[it, s, ch], across)
        for k in near_first[::-1]:
            zs[it, s, k, :, cols] = (xo[s, up(k), :, cols] + xr[it, s, up(k), :, cols].astype(F32)).astype(BF16)
            send(
                zs.at[it, s, k, :, cols], zr.at[it, s, k, :, cols],
                rz_s.at[it, s, ch, k], rz_r.at[it, s, ch, k], dev(up(k), x, c),
            )
        zo[s, :, cols] = xo[s, z, :, cols] + xr[it, s, z, :, cols].astype(F32)

    def rs_end(it, s):
        for ch in range(CHUNKS):
            cols = pl.ds(ch * width, width)
            total = zo[s, :, cols]
            for k in near_first:
                arrived(zr.at[it, s, k, :, cols], rz_s.at[it, s, ch, k], rz_r.at[it, s, ch, k], dev(down(k), x, c))
                total = total + zr[it, s, k, :, cols].astype(F32)
            new = 0.4 * resp[s, :, cols] + 0.6 * (rhs[:, s, cols] - total) / denom[:, cols]
            if it == ITERS - 1:
                out[:, s, cols] = new
            else:
                resp[s, :, cols] = new

    a, b = 0, 1
    ag_start(0, a)
    ag_start(0, b)
    ag_z(0, a)
    ag_x(0, a)
    ag_z(0, b)
    ag_c(0, a)
    loads[0].wait()
    for it in range(ITERS):
        halves(it, a)
        if it == 0:
            for load in loads[1:]:
                load.wait()
        else:
            ag_z(it, b)
        exchange(it, a, 0)
        ag_x(it, b)
        exchange(it, a, 1)
        rs_x(it, a, 0)
        ag_c(it, b)
        halves(it, b)
        rs_x(it, a, 1)
        rs_z(it, a, 0)
        exchange(it, b, 0)
        rs_z(it, a, 1)
        rs_x(it, b, 0)
        exchange(it, b, 1)
        rs_end(it, a)
        if it + 1 < ITERS:
            ag_start(it + 1, a)
        rs_x(it, b, 1)
        rs_z(it, b, 0)
        rs_z(it, b, 1)
        if it + 1 < ITERS:
            ag_z(it + 1, a)
        rs_end(it, b)
        if it + 1 < ITERS:
            ag_start(it + 1, b)
            ag_x(it + 1, a)
            ag_c(it + 1, a)
    for copy in sent:
        copy.wait_send()


def fused(rhs, occ_energy, vir_energy, occ_ints, vir_ints, devices):
    rows, states, nvir = rhs.shape
    local_aux, nocc, _ = occ_ints.shape
    nz = devices // 4
    dma = pltpu.SemaphoreType.DMA
    vmem = pl.BlockSpec(memory_space=pltpu.VMEM)
    hbm = pl.BlockSpec(memory_space=pl.ANY)
    lead = (ITERS, states)
    pair = lambda *shape: [dma(lead + shape)] * 2
    flops = ITERS * 2 * local_aux * nocc * states * nvir * (nocc + nvir)
    return pl.pallas_call(
        functools.partial(kernel, nz),
        out_shape=jax.ShapeDtypeStruct(rhs.shape, F32),
        in_specs=[vmem, vmem, vmem, hbm, hbm],
        out_specs=vmem,
        scratch_shapes=[
            pltpu.VMEM(occ_ints.shape, BF16),
            pltpu.VMEM((nvir, local_aux * nvir), BF16),
            pltpu.VMEM((rows, nvir), F32),
            pltpu.VMEM((states, rows, nvir), F32),
            pltpu.VMEM(lead + (nz, 2, 2, rows, nvir), BF16),
            pltpu.VMEM((nocc, local_aux * nvir), BF16),
            pltpu.VMEM(lead + (nz, 2, 2, rows, nvir), F32),
            pltpu.VMEM(lead + (nz, 2, rows, nvir), F32),
            pltpu.VMEM((states, nz, rows, nvir), F32),
            pltpu.VMEM(lead + (nz, rows, nvir), BF16),
            pltpu.VMEM(lead + (nz, rows, nvir), BF16),
            pltpu.VMEM((states, rows, nvir), F32),
            pltpu.VMEM(lead + (nz, rows, nvir), BF16),
            pltpu.VMEM(lead + (nz, rows, nvir), BF16),
            dma((local_aux + 1,)),
            *pair(nz), *pair(nz), *pair(2),
            *pair(CHUNKS), *pair(CHUNKS), *pair(CHUNKS, nz),
        ],
        compiler_params=pltpu.CompilerParams(
            collective_id=0, has_side_effects=True, vmem_limit_bytes=52 * 2**20
        ),
        cost_estimate=pl.CostEstimate(flops=flops, bytes_accessed=2 * vir_ints.size, transcendentals=0),
    )(rhs, occ_energy.reshape(1, nocc), vir_energy.reshape(1, nvir), occ_ints, vir_ints)


def collective(rhs, occ_energy, vir_energy, occ_ints, vir_ints):
    own_rows, states, nvir = rhs.shape
    local_aux, nocc, _ = occ_ints.shape
    position = lax.axis_index("aux")
    my_occ = lax.dynamic_slice_in_dim(occ_energy, position * own_rows, own_rows, 0)
    denom = vir_energy[None, None, :] - my_occ[:, None, None]
    response = rhs / denom
    for step in range(ITERS):
        rounded = response.astype(BF16)
        piece = lax.all_gather(rounded, "aux", axis=0, tiled=True)
        flat = piece.reshape(piece.shape[0], states * nvir)
        half = jnp.einsum("pij,jk->pik", occ_ints, flat, preferred_element_type=F32)
        half = half.astype(BF16).reshape(local_aux, nocc, states, nvir)
        exchange = lax.psum_scatter(
            lax.dot_general(half, vir_ints, (((0, 3), (0, 2)), ((), ())), preferred_element_type=F32),
            "aux", scatter_dimension=0, tiled=True,
        )
        response = 0.4 * response + 0.6 * (rhs - exchange) / denom
    return response


def solution(mesh):
    devices = mesh.shape["aux"]

    def shards(rhs, occ_energy, vir_energy, occ_ints, vir_ints):
        rows, states, nvir = rhs.shape
        if rows % 16 == 0 and devices % 4 == 0 and devices > 4 and states == 2:
            return fused(rhs, occ_energy, vir_energy, occ_ints, vir_ints, devices)
        return collective(rhs, occ_energy, vir_energy, occ_ints, vir_ints)

    split = P(("grp", "aux"), None, None)
    return jax.shard_map(
        shards, mesh=mesh, in_specs=(split, P("grp"), P("grp"), split, split), out_specs=split, check_vma=False
    )
```

```python
import functools

import jax
import jax.numpy as jnp
from jax import lax
from jax.experimental import pallas as pl
from jax.experimental.pallas import tpu as pltpu
from jax.sharding import PartitionSpec as P

ITERS = 2
CHUNKS = 2
MESH = pl.DeviceIdType.MESH
F32 = jnp.float32
BF16 = jnp.bfloat16


def kernel(
    nz, rhs_hbm, occ_e_hbm, vir_e_hbm, occ_hbm, vir_hbm, out,
    rhs, occ_e, vir_e, occ_v, vir_v, vir_t, denom, resp, ag, half, ex, cr, xo, xs, xr, zo, zs, zr,
    load_sem, agz_s, agz_r, agx_s, agx_r, agc_s, agc_r,
    rc_s, rc_r, rx_s, rx_r, rz_s, rz_r,
):
    rows, states, nvir = rhs.shape
    nocc = half.shape[0]
    local_aux = occ_v.shape[0]
    width = nvir // CHUNKS
    grp = lax.axis_index("grp")
    me = lax.axis_index("aux")
    c = lax.rem(me, 2)
    x = lax.rem(me // 2, 2)
    z = me // 4

    def dev(zz, xx, cc):
        return (grp, (zz * 2 + xx) * 2 + cc)

    def up(k):
        return lax.rem(z + k, nz)

    def down(k):
        return lax.rem(z + nz - k, nz)

    sibling = dev(z, x, 1 - c)
    across = dev(z, 1 - x, c)

    pairs = [(rhs_hbm, rhs), (occ_e_hbm, occ_e), (vir_e_hbm, vir_e), (occ_hbm, occ_v)]
    pairs += [(vir_hbm.at[p], vir_v.at[p]) for p in range(local_aux)]
    loads = [pltpu.make_async_copy(src, dst, load_sem.at[i]) for i, (src, dst) in enumerate(pairs)]
    for load in loads:
        load.start()

    barrier = pltpu.get_barrier_semaphore()
    for peer in [sibling, across] + [dev(up(k), x, c) for k in range(1, nz)]:
        pl.semaphore_signal(barrier, inc=1, device_id=peer, device_id_type=MESH)

    for load in loads[:3]:
        load.wait()
    picked = lax.broadcasted_iota(jnp.int32, (rows, nocc), 1) == (
        lax.broadcasted_iota(jnp.int32, (rows, nocc), 0) + me * rows
    )
    own_occ = jnp.sum(jnp.where(picked, occ_e[...], 0.0), axis=1, keepdims=True)
    denom[...] = vir_e[...] - own_occ
    for s in range(states):
        resp[s] = rhs[:, s, :] / denom[...]
    pl.semaphore_wait(barrier, nz + 1)

    sent = []

    def send(src, dst, s_sem, r_sem, to):
        copy = pltpu.make_async_remote_copy(
            src_ref=src, dst_ref=dst, send_sem=s_sem, recv_sem=r_sem, device_id=to, device_id_type=MESH
        )
        copy.start()
        sent.append(copy)

    def arrived(dst, s_sem, r_sem, frm):
        pltpu.make_async_remote_copy(
            src_ref=dst, dst_ref=dst, send_sem=s_sem, recv_sem=r_sem, device_id=frm, device_id_type=MESH
        ).wait_recv()

    near_first = sorted(range(1, nz), key=lambda k: min(k, nz - k))

    def ag_start(it, s):
        block = ag.at[it, s, z, x, c]
        block[...] = resp[s].astype(BF16)
        for k in near_first:
            send(block, block, agz_s.at[it, s, k], agz_r.at[it, s, k], dev(up(k), x, c))
        send(block, block, agx_s.at[it, s, 0], agx_r.at[it, s, 0], across)

    def ag_z(it, s):
        for k in near_first:
            block = ag.at[it, s, down(k), x, c]
            arrived(block, agz_s.at[it, s, k], agz_r.at[it, s, k], dev(down(k), x, c))
            send(block, block, agx_s.at[it, s, k], agx_r.at[it, s, k], across)
        line = ag.at[it, s, :, x, c]
        send(line, line, agc_s.at[it, s, 0], agc_r.at[it, s, 0], sibling)

    def ag_x(it, s):
        for k in [0] + near_first:
            block = ag.at[it, s, down(k), 1 - x, c]
            arrived(block, agx_s.at[it, s, k], agx_r.at[it, s, k], across)
        line = ag.at[it, s, :, 1 - x, c]
        send(line, line, agc_s.at[it, s, 1], agc_r.at[it, s, 1], sibling)

    def ag_c(it, s):
        arrived(ag.at[it, s, :, x, 1 - c], agc_s.at[it, s, 0], agc_r.at[it, s, 0], sibling)
        arrived(ag.at[it, s, :, 1 - x, 1 - c], agc_s.at[it, s, 1], agc_r.at[it, s, 1], sibling)

    def halves(it, s):
        gathered = ag[it, s].reshape(nocc, nvir)
        product = jnp.dot(occ_v[...].reshape(local_aux * nocc, nocc), gathered, preferred_element_type=F32)
        for p in range(local_aux):
            half[:, pl.ds(p * nvir, nvir)] = product[p * nocc : (p + 1) * nocc].astype(BF16)

    def turn(p):
        loads[4 + p].wait()
        vir_t[pl.ds(p * nvir, nvir), :] = vir_v[p].T

    def exchange(it, s, ch):
        cols = pl.ds(ch * width, width)
        product = jnp.dot(half[...], vir_t[:, cols], preferred_element_type=F32)
        ex[it, s, :, :, :, :, cols] = product.reshape(nz, 2, 2, rows, width)
        send(
            ex.at[it, s, :, :, 1 - c, :, cols], cr.at[it, s, :, :, :, cols],
            rc_s.at[it, s, ch], rc_r.at[it, s, ch], sibling,
        )

    def rs_x(it, s, ch):
        cols = pl.ds(ch * width, width)
        arrived(cr.at[it, s, :, :, :, cols], rc_s.at[it, s, ch], rc_r.at[it, s, ch], sibling)
        xs[it, s, :, :, cols] = (
            ex[it, s, :, 1 - x, c, :, cols] + cr[it, s, :, 1 - x, :, cols]
        ).astype(BF16)
        send(
            xs.at[it, s, :, :, cols], xr.at[it, s, :, :, cols],
            rx_s.at[it, s, ch], rx_r.at[it, s, ch], across,
        )
        xo[s, :, :, cols] = ex[it, s, :, x, c, :, cols] + cr[it, s, :, x, :, cols]

    def rs_z(it, s, ch):
        cols = pl.ds(ch * width, width)
        arrived(xr.at[it, s, :, :, cols], rx_s.at[it, s, ch], rx_r.at[it, s, ch], across)
        for k in near_first[::-1]:
            zs[it, s, k, :, cols] = (xo[s, up(k), :, cols] + xr[it, s, up(k), :, cols].astype(F32)).astype(BF16)
            send(
                zs.at[it, s, k, :, cols], zr.at[it, s, k, :, cols],
                rz_s.at[it, s, ch, k], rz_r.at[it, s, ch, k], dev(up(k), x, c),
            )
        zo[s, :, cols] = xo[s, z, :, cols] + xr[it, s, z, :, cols].astype(F32)

    def rs_end(it, s):
        for ch in range(CHUNKS):
            cols = pl.ds(ch * width, width)
            total = zo[s, :, cols]
            for k in near_first:
                arrived(zr.at[it, s, k, :, cols], rz_s.at[it, s, ch, k], rz_r.at[it, s, ch, k], dev(down(k), x, c))
                total = total + zr[it, s, k, :, cols].astype(F32)
            new = 0.4 * resp[s, :, cols] + 0.6 * (rhs[:, s, cols] - total) / denom[:, cols]
            if it == ITERS - 1:
                out[:, s, cols] = new
            else:
                resp[s, :, cols] = new

    a, b = 0, 1
    ag_start(0, a)
    ag_start(0, b)
    first, second = local_aux // 2, local_aux
    for p in range(first):
        turn(p)
    ag_z(0, a)
    for p in range(first, second):
        turn(p)
    ag_x(0, a)
    ag_z(0, b)
    ag_c(0, a)
    loads[3].wait()
    for it in range(ITERS):
        halves(it, a)
        if it > 0:
            ag_z(it, b)
        exchange(it, a, 0)
        ag_x(it, b)
        exchange(it, a, 1)
        rs_x(it, a, 0)
        ag_c(it, b)
        halves(it, b)
        rs_x(it, a, 1)
        rs_z(it, a, 0)
        exchange(it, b, 0)
        rs_z(it, a, 1)
        rs_x(it, b, 0)
        exchange(it, b, 1)
        rs_end(it, a)
        if it + 1 < ITERS:
            ag_start(it + 1, a)
        rs_x(it, b, 1)
        rs_z(it, b, 0)
        rs_z(it, b, 1)
        if it + 1 < ITERS:
            ag_z(it + 1, a)
        rs_end(it, b)
        if it + 1 < ITERS:
            ag_start(it + 1, b)
            ag_x(it + 1, a)
            ag_c(it + 1, a)
    for copy in sent:
        copy.wait_send()


def fused(rhs, occ_energy, vir_energy, occ_ints, vir_ints, devices):
    rows, states, nvir = rhs.shape
    local_aux, nocc, _ = occ_ints.shape
    nz = devices // 4
    dma = pltpu.SemaphoreType.DMA
    vmem = pl.BlockSpec(memory_space=pltpu.VMEM)
    hbm = pl.BlockSpec(memory_space=pltpu.HBM)
    lead = (ITERS, states)
    pair = lambda *shape: [dma(lead + shape)] * 2
    flops = ITERS * 2 * local_aux * nocc * states * nvir * (nocc + nvir)
    return pl.pallas_call(
        functools.partial(kernel, nz),
        out_shape=jax.ShapeDtypeStruct(rhs.shape, F32),
        in_specs=[hbm] * 5,
        out_specs=vmem,
        scratch_shapes=[
            pltpu.VMEM(rhs.shape, F32),
            pltpu.VMEM((1, nocc), F32),
            pltpu.VMEM((1, nvir), F32),
            pltpu.VMEM(occ_ints.shape, BF16),
            pltpu.VMEM(vir_ints.shape, BF16),
            pltpu.VMEM((local_aux * nvir, nvir), BF16),
            pltpu.VMEM((rows, nvir), F32),
            pltpu.VMEM((states, rows, nvir), F32),
            pltpu.VMEM(lead + (nz, 2, 2, rows, nvir), BF16),
            pltpu.VMEM((nocc, local_aux * nvir), BF16),
            pltpu.VMEM(lead + (nz, 2, 2, rows, nvir), F32),
            pltpu.VMEM(lead + (nz, 2, rows, nvir), F32),
            pltpu.VMEM((states, nz, rows, nvir), F32),
            pltpu.VMEM(lead + (nz, rows, nvir), BF16),
            pltpu.VMEM(lead + (nz, rows, nvir), BF16),
            pltpu.VMEM((states, rows, nvir), F32),
            pltpu.VMEM(lead + (nz, rows, nvir), BF16),
            pltpu.VMEM(lead + (nz, rows, nvir), BF16),
            dma((local_aux + 4,)),
            *pair(nz), *pair(nz), *pair(2),
            *pair(CHUNKS), *pair(CHUNKS), *pair(CHUNKS, nz),
        ],
        compiler_params=pltpu.CompilerParams(
            collective_id=0, has_side_effects=True, vmem_limit_bytes=52 * 2**20
        ),
        cost_estimate=pl.CostEstimate(flops=flops, bytes_accessed=2 * vir_ints.size, transcendentals=0),
    )(rhs, occ_energy.reshape(1, nocc), vir_energy.reshape(1, nvir), occ_ints, vir_ints)


def collective(rhs, occ_energy, vir_energy, occ_ints, vir_ints):
    own_rows, states, nvir = rhs.shape
    local_aux, nocc, _ = occ_ints.shape
    position = lax.axis_index("aux")
    my_occ = lax.dynamic_slice_in_dim(occ_energy, position * own_rows, own_rows, 0)
    denom = vir_energy[None, None, :] - my_occ[:, None, None]
    response = rhs / denom
    for step in range(ITERS):
        rounded = response.astype(BF16)
        piece = lax.all_gather(rounded, "aux", axis=0, tiled=True)
        flat = piece.reshape(piece.shape[0], states * nvir)
        half = jnp.einsum("pij,jk->pik", occ_ints, flat, preferred_element_type=F32)
        half = half.astype(BF16).reshape(local_aux, nocc, states, nvir)
        exchange = lax.psum_scatter(
            lax.dot_general(half, vir_ints, (((0, 3), (0, 2)), ((), ())), preferred_element_type=F32),
            "aux", scatter_dimension=0, tiled=True,
        )
        response = 0.4 * response + 0.6 * (rhs - exchange) / denom
    return response


def solution(mesh):
    devices = mesh.shape["aux"]

    def shards(rhs, occ_energy, vir_energy, occ_ints, vir_ints):
        rows, states, nvir = rhs.shape
        if rows % 16 == 0 and devices % 4 == 0 and devices > 4 and states == 2:
            return fused(rhs, occ_energy, vir_energy, occ_ints, vir_ints, devices)
        return collective(rhs, occ_energy, vir_energy, occ_ints, vir_ints)

    split = P(("grp", "aux"), None, None)
    return jax.shard_map(
        shards, mesh=mesh, in_specs=(split, P("grp"), P("grp"), split, split), out_specs=split, check_vma=False
    )
```

```python
import functools

import jax
import jax.numpy as jnp
from jax import lax
from jax.experimental import pallas as pl
from jax.experimental.pallas import tpu as pltpu
from jax.sharding import PartitionSpec as P

ITERS = 2
CHUNKS = 2
MESH = pl.DeviceIdType.MESH
F32 = jnp.float32
BF16 = jnp.bfloat16


def kernel(
    nz, rhs_hbm, occ_e_hbm, vir_e_hbm, occ_hbm, vir_hbm, out,
    rhs, occ_e, vir_e, occ_v, vir_v, denom, resp, ag, half, ex, cr, xo, xs, xr, zo, zs, zr,
    load_sem, agz_s, agz_r, agx_s, agx_r, agc_s, agc_r,
    rc_s, rc_r, rx_s, rx_r, rz_s, rz_r,
):
    rows, states, nvir = rhs.shape
    nocc = half.shape[1]
    local_aux = occ_v.shape[0]
    width = nvir // CHUNKS
    grp = lax.axis_index("grp")
    me = lax.axis_index("aux")
    c = lax.rem(me, 2)
    x = lax.rem(me // 2, 2)
    z = me // 4

    def dev(zz, xx, cc):
        return (grp, (zz * 2 + xx) * 2 + cc)

    def up(k):
        return lax.rem(z + k, nz)

    def down(k):
        return lax.rem(z + nz - k, nz)

    sibling = dev(z, x, 1 - c)
    across = dev(z, 1 - x, c)

    pairs = [(rhs_hbm, rhs), (occ_e_hbm, occ_e), (vir_e_hbm, vir_e), (occ_hbm, occ_v)]
    pairs += [(vir_hbm.at[p], vir_v.at[:, pl.ds(p * nvir, nvir)]) for p in range(local_aux)]
    loads = [pltpu.make_async_copy(src, dst, load_sem.at[i]) for i, (src, dst) in enumerate(pairs)]
    for load in loads:
        load.start()

    barrier = pltpu.get_barrier_semaphore()
    for peer in [sibling, across] + [dev(up(k), x, c) for k in range(1, nz)]:
        pl.semaphore_signal(barrier, inc=1, device_id=peer, device_id_type=MESH)

    for load in loads[:3]:
        load.wait()
    picked = lax.broadcasted_iota(jnp.int32, (rows, nocc), 1) == (
        lax.broadcasted_iota(jnp.int32, (rows, nocc), 0) + me * rows
    )
    own_occ = jnp.sum(jnp.where(picked, occ_e[...], 0.0), axis=1, keepdims=True)
    denom[...] = vir_e[...] - own_occ
    for s in range(states):
        resp[s] = rhs[:, s, :] / denom[...]
    pl.semaphore_wait(barrier, nz + 1)

    sent = []

    def send(src, dst, s_sem, r_sem, to):
        copy = pltpu.make_async_remote_copy(
            src_ref=src, dst_ref=dst, send_sem=s_sem, recv_sem=r_sem, device_id=to, device_id_type=MESH
        )
        copy.start()
        sent.append(copy)

    def arrived(dst, s_sem, r_sem, frm):
        pltpu.make_async_remote_copy(
            src_ref=dst, dst_ref=dst, send_sem=s_sem, recv_sem=r_sem, device_id=frm, device_id_type=MESH
        ).wait_recv()

    near_first = sorted(range(1, nz), key=lambda k: min(k, nz - k))

    def ag_start(it, s, ch):
        cols = pl.ds(ch * width, width)
        block = ag.at[it, s, z, x, c, :, cols]
        block[...] = resp[s, :, cols].astype(BF16)
        for k in near_first[::-1]:
            send(block, block, agz_s.at[it, s, ch, k], agz_r.at[it, s, ch, k], dev(up(k), x, c))
        send(block, block, agx_s.at[it, s, ch, 0], agx_r.at[it, s, ch, 0], across)

    def ag_z(it, s, ch):
        cols = pl.ds(ch * width, width)
        for k in near_first:
            block = ag.at[it, s, down(k), x, c, :, cols]
            arrived(block, agz_s.at[it, s, ch, k], agz_r.at[it, s, ch, k], dev(down(k), x, c))
            send(block, block, agx_s.at[it, s, ch, k], agx_r.at[it, s, ch, k], across)
        line = ag.at[it, s, :, x, c, :, cols]
        send(line, line, agc_s.at[it, s, ch, 0], agc_r.at[it, s, ch, 0], sibling)

    def ag_x(it, s, ch):
        cols = pl.ds(ch * width, width)
        for k in [0] + near_first:
            block = ag.at[it, s, down(k), 1 - x, c, :, cols]
            arrived(block, agx_s.at[it, s, ch, k], agx_r.at[it, s, ch, k], across)
        line = ag.at[it, s, :, 1 - x, c, :, cols]
        send(line, line, agc_s.at[it, s, ch, 1], agc_r.at[it, s, ch, 1], sibling)

    def halves(it, s, ch):
        cols = pl.ds(ch * width, width)
        arrived(ag.at[it, s, :, x, 1 - c, :, cols], agc_s.at[it, s, ch, 0], agc_r.at[it, s, ch, 0], sibling)
        arrived(ag.at[it, s, :, 1 - x, 1 - c, :, cols], agc_s.at[it, s, ch, 1], agc_r.at[it, s, ch, 1], sibling)
        if not ready[0]:
            ready[0] = True
            loads[3].wait()
        gathered = ag[it, s, :, :, :, :, cols].reshape(nocc, width)
        product = jnp.dot(occ_v[...].reshape(local_aux * nocc, nocc), gathered, preferred_element_type=F32)
        for p in range(local_aux):
            half[s, :, pl.ds(p * nvir + ch * width, width)] = product[p * nocc : (p + 1) * nocc].astype(BF16)

    def exchange(it, s, ch):
        cols = pl.ds(ch * width, width)
        if not ready[1]:
            ready[1] = True
            for load in loads[4:]:
                load.wait()
        product = lax.dot_general(
            half[s], vir_v[cols, :], (((1,), (1,)), ((), ())), preferred_element_type=F32
        )
        ex[it, s, :, :, :, :, cols] = product.reshape(nz, 2, 2, rows, width)
        send(
            ex.at[it, s, :, :, 1 - c, :, cols], cr.at[it, s, :, :, :, cols],
            rc_s.at[it, s, ch], rc_r.at[it, s, ch], sibling,
        )

    def rs_x(it, s, ch):
        cols = pl.ds(ch * width, width)
        arrived(cr.at[it, s, :, :, :, cols], rc_s.at[it, s, ch], rc_r.at[it, s, ch], sibling)
        xs[it, s, :, :, cols] = (
            ex[it, s, :, 1 - x, c, :, cols] + cr[it, s, :, 1 - x, :, cols]
        ).astype(BF16)
        send(
            xs.at[it, s, :, :, cols], xr.at[it, s, :, :, cols],
            rx_s.at[it, s, ch], rx_r.at[it, s, ch], across,
        )
        xo[s, :, :, cols] = ex[it, s, :, x, c, :, cols] + cr[it, s, :, x, :, cols]

    def rs_z(it, s, ch):
        cols = pl.ds(ch * width, width)
        arrived(xr.at[it, s, :, :, cols], rx_s.at[it, s, ch], rx_r.at[it, s, ch], across)
        for k in near_first[::-1]:
            zs[it, s, k, :, cols] = (xo[s, up(k), :, cols] + xr[it, s, up(k), :, cols].astype(F32)).astype(BF16)
            send(
                zs.at[it, s, k, :, cols], zr.at[it, s, k, :, cols],
                rz_s.at[it, s, ch, k], rz_r.at[it, s, ch, k], dev(up(k), x, c),
            )
        zo[s, :, cols] = xo[s, z, :, cols] + xr[it, s, z, :, cols].astype(F32)

    def update(it, s, ch):
        cols = pl.ds(ch * width, width)
        total = zo[s, :, cols]
        for k in near_first:
            arrived(zr.at[it, s, k, :, cols], rz_s.at[it, s, ch, k], rz_r.at[it, s, ch, k], dev(down(k), x, c))
            total = total + zr[it, s, k, :, cols].astype(F32)
        new = 0.4 * resp[s, :, cols] + 0.6 * (rhs[:, s, cols] - total) / denom[:, cols]
        if it == ITERS - 1:
            out[:, s, cols] = new
        else:
            resp[s, :, cols] = new
            ag_start(it + 1, s, ch)

    ready = [False, False]
    steps = dict(
        ag_start=ag_start, ag_z=ag_z, ag_x=ag_x, halves=halves,
        exchange=exchange, rs_x=rs_x, rs_z=rs_z, update=update,
    )
    for name, it, s, ch in plan(states):
        steps[name](it, s, ch)
    for copy in sent:
        copy.wait_send()


def plan(states):
    units = states * CHUNKS
    link, core, hop, near = 10500 // units // 2, 1800 // units, 1000, 700
    took = dict(
        ag_start=150, ag_z=200, ag_x=100, halves=1100 // units,
        exchange=4400 // units, rs_x=200, rs_z=200, update=250,
    )
    free, order, now = dict(x=0, z=0, c=0), [], 0

    def carry(lane, begin, length, latency):
        free[lane] = max(free[lane], begin) + length
        return free[lane] + latency

    todo = [("ag_start", 0, s, ch) for s in range(states) for ch in range(CHUNKS)]
    for it in range(ITERS):
        for name in ("ag_z", "ag_x", "halves", "exchange", "rs_x", "rs_z", "update"):
            todo += [(name, it, s, ch) for s in range(states) for ch in range(CHUNKS)]
    arrival = {}
    done = set()
    while todo:

        def rank(step):
            name, it, s, ch = step
            if name == "exchange":
                needs = [("halves", it, s, each) in done for each in range(CHUNKS)]
                begin = 0 if all(needs) else 1 << 40
            else:
                begin = 0 if name == "ag_start" else arrival.get(step, 1 << 40)
            return (max(now, begin), name in ("halves", "exchange"), s, it, ch)

        step = min(todo, key=rank)
        name, it, s, ch = step
        now = max(now, rank(step)[0]) + took[name]
        todo.remove(step)
        done.add(step)
        order.append(step)
        if name == "ag_start" or (name == "update" and it + 1 < ITERS):
            ahead = it + (name == "update")
            arrival[("ag_z", ahead, s, ch)] = carry("z", now, link, hop)
            carry("x", now, link // 4, hop)
        elif name == "ag_z":
            arrival[("ag_x", it, s, ch)] = carry("x", now, link * 3 // 4, hop)
        elif name == "ag_x":
            arrival[("halves", it, s, ch)] = carry("c", now, core // 4, near)
        elif name == "exchange":
            arrival[("rs_x", it, s, ch)] = carry("c", now, core, near)
        elif name == "rs_x":
            arrival[("rs_z", it, s, ch)] = carry("x", now, link, hop)
        elif name == "rs_z":
            arrival[("update", it, s, ch)] = carry("z", now, link, hop)
    return order


def fused(rhs, occ_energy, vir_energy, occ_ints, vir_ints, devices):
    rows, states, nvir = rhs.shape
    local_aux, nocc, _ = occ_ints.shape
    nz = devices // 4
    dma = pltpu.SemaphoreType.DMA
    vmem = pl.BlockSpec(memory_space=pltpu.VMEM)
    hbm = pl.BlockSpec(memory_space=pltpu.HBM)
    lead = (ITERS, states)
    pair = lambda *shape: [dma(lead + shape)] * 2
    flops = ITERS * 2 * local_aux * nocc * states * nvir * (nocc + nvir)
    return pl.pallas_call(
        functools.partial(kernel, nz),
        out_shape=jax.ShapeDtypeStruct(rhs.shape, F32),
        in_specs=[hbm] * 5,
        out_specs=vmem,
        scratch_shapes=[
            pltpu.VMEM(rhs.shape, F32),
            pltpu.VMEM((1, nocc), F32),
            pltpu.VMEM((1, nvir), F32),
            pltpu.VMEM(occ_ints.shape, BF16),
            pltpu.VMEM((nvir, local_aux * nvir), BF16),
            pltpu.VMEM((rows, nvir), F32),
            pltpu.VMEM((states, rows, nvir), F32),
            pltpu.VMEM(lead + (nz, 2, 2, rows, nvir), BF16),
            pltpu.VMEM((states, nocc, local_aux * nvir), BF16),
            pltpu.VMEM(lead + (nz, 2, 2, rows, nvir), F32),
            pltpu.VMEM(lead + (nz, 2, rows, nvir), F32),
            pltpu.VMEM((states, nz, rows, nvir), F32),
            pltpu.VMEM(lead + (nz, rows, nvir), BF16),
            pltpu.VMEM(lead + (nz, rows, nvir), BF16),
            pltpu.VMEM((states, rows, nvir), F32),
            pltpu.VMEM(lead + (nz, rows, nvir), BF16),
            pltpu.VMEM(lead + (nz, rows, nvir), BF16),
            dma((local_aux + 4,)),
            *pair(CHUNKS, nz), *pair(CHUNKS, nz), *pair(CHUNKS, 2),
            *pair(CHUNKS), *pair(CHUNKS), *pair(CHUNKS, nz),
        ],
        compiler_params=pltpu.CompilerParams(
            collective_id=0, has_side_effects=True, vmem_limit_bytes=62 * 2**20
        ),
        cost_estimate=pl.CostEstimate(flops=flops, bytes_accessed=2 * vir_ints.size, transcendentals=0),
    )(rhs, occ_energy.reshape(1, nocc), vir_energy.reshape(1, nvir), occ_ints, vir_ints)


def collective(rhs, occ_energy, vir_energy, occ_ints, vir_ints):
    own_rows, states, nvir = rhs.shape
    local_aux, nocc, _ = occ_ints.shape
    position = lax.axis_index("aux")
    my_occ = lax.dynamic_slice_in_dim(occ_energy, position * own_rows, own_rows, 0)
    denom = vir_energy[None, None, :] - my_occ[:, None, None]
    response = rhs / denom
    for step in range(ITERS):
        rounded = response.astype(BF16)
        piece = lax.all_gather(rounded, "aux", axis=0, tiled=True)
        flat = piece.reshape(piece.shape[0], states * nvir)
        half = jnp.einsum("pij,jk->pik", occ_ints, flat, preferred_element_type=F32)
        half = half.astype(BF16).reshape(local_aux, nocc, states, nvir)
        exchange = lax.psum_scatter(
            lax.dot_general(half, vir_ints, (((0, 3), (0, 2)), ((), ())), preferred_element_type=F32),
            "aux", scatter_dimension=0, tiled=True,
        )
        response = 0.4 * response + 0.6 * (rhs - exchange) / denom
    return response


def solution(mesh):
    devices = mesh.shape["aux"]

    def shards(rhs, occ_energy, vir_energy, occ_ints, vir_ints):
        rows, states, nvir = rhs.shape
        if rows % 16 == 0 and devices % 4 == 0 and devices > 4 and states == 2:
            return fused(rhs, occ_energy, vir_energy, occ_ints, vir_ints, devices)
        return collective(rhs, occ_energy, vir_energy, occ_ints, vir_ints)

    split = P(("grp", "aux"), None, None)
    return jax.shard_map(
        shards, mesh=mesh, in_specs=(split, P("grp"), P("grp"), split, split), out_specs=split, check_vma=False
    )
```

```python
import functools

import jax
import jax.numpy as jnp
from jax import lax
from jax.experimental import pallas as pl
from jax.experimental.pallas import tpu as pltpu
from jax.sharding import PartitionSpec as P

ITERS = 2
CHUNKS = 1
MESH = pl.DeviceIdType.MESH
F32 = jnp.float32
BF16 = jnp.bfloat16


def kernel(
    nz, rhs_hbm, occ_e_hbm, vir_e_hbm, occ_hbm, vir_hbm, out,
    rhs, occ_e, vir_e, occ_v, vir_v, denom, right, resp, ag, half, ex, cr, xo, xs, xr, zo, zs, zr,
    load_sem, agz_s, agz_r, agx_s, agx_r, agc_s, agc_r,
    rc_s, rc_r, rx_s, rx_r, rz_s, rz_r,
):
    rows, states, nvir = rhs.shape
    nocc = half.shape[1]
    local_aux = occ_v.shape[0]
    width = nvir // CHUNKS
    grp = lax.axis_index("grp")
    me = lax.axis_index("aux")
    c = lax.rem(me, 2)
    x = lax.rem(me // 2, 2)
    z = me // 4

    def dev(zz, xx, cc):
        return (grp, (zz * 2 + xx) * 2 + cc)

    def up(k):
        return lax.rem(z + k, nz)

    def down(k):
        return lax.rem(z + nz - k, nz)

    sibling = dev(z, x, 1 - c)
    across = dev(z, 1 - x, c)

    pairs = [(rhs_hbm, rhs), (occ_e_hbm, occ_e), (vir_e_hbm, vir_e), (occ_hbm, occ_v)]
    pairs += [(vir_hbm.at[p], vir_v.at[:, pl.ds(p * nvir, nvir)]) for p in range(local_aux)]
    loads = [pltpu.make_async_copy(src, dst, load_sem.at[i]) for i, (src, dst) in enumerate(pairs)]
    for load in loads:
        load.start()

    barrier = pltpu.get_barrier_semaphore()
    for peer in [sibling, across] + [dev(up(k), x, c) for k in range(1, nz)]:
        pl.semaphore_signal(barrier, inc=1, device_id=peer, device_id_type=MESH)

    for load in loads[:3]:
        load.wait()
    picked = lax.broadcasted_iota(jnp.int32, (rows, nocc), 1) == (
        lax.broadcasted_iota(jnp.int32, (rows, nocc), 0) + me * rows
    )
    own_occ = jnp.sum(jnp.where(picked, occ_e[...], 0.0), axis=1, keepdims=True)
    denom[...] = vir_e[...] - own_occ
    for s in range(states):
        right[s] = rhs[:, s, :]
        resp[s] = right[s] / denom[...]
    pl.semaphore_wait(barrier, nz + 1)

    sent = []

    def send(src, dst, s_sem, r_sem, to):
        copy = pltpu.make_async_remote_copy(
            src_ref=src, dst_ref=dst, send_sem=s_sem, recv_sem=r_sem, device_id=to, device_id_type=MESH
        )
        copy.start()
        sent.append(copy)

    def arrived(dst, s_sem, r_sem, frm):
        pltpu.make_async_remote_copy(
            src_ref=dst, dst_ref=dst, send_sem=s_sem, recv_sem=r_sem, device_id=frm, device_id_type=MESH
        ).wait_recv()

    near_first = sorted(range(1, nz), key=lambda k: min(k, nz - k))

    def ag_start(it, s, ch):
        cols = pl.ds(ch * width, width)
        block = ag.at[it, s, z, x, c, :, cols]
        block[...] = resp[s, :, cols].astype(BF16)
        for k in near_first[::-1]:
            send(block, block, agz_s.at[it, s, ch, k], agz_r.at[it, s, ch, k], dev(up(k), x, c))
        send(block, block, agx_s.at[it, s, ch, 0], agx_r.at[it, s, ch, 0], across)

    def ag_z(it, s, ch):
        cols = pl.ds(ch * width, width)
        for k in near_first:
            block = ag.at[it, s, down(k), x, c, :, cols]
            arrived(block, agz_s.at[it, s, ch, k], agz_r.at[it, s, ch, k], dev(down(k), x, c))
            send(block, block, agx_s.at[it, s, ch, k], agx_r.at[it, s, ch, k], across)
        line = ag.at[it, s, :, x, c, :, cols]
        send(line, line, agc_s.at[it, s, ch, 0], agc_r.at[it, s, ch, 0], sibling)

    def ag_x(it, s, ch):
        cols = pl.ds(ch * width, width)
        for k in [0] + near_first:
            block = ag.at[it, s, down(k), 1 - x, c, :, cols]
            arrived(block, agx_s.at[it, s, ch, k], agx_r.at[it, s, ch, k], across)
        line = ag.at[it, s, :, 1 - x, c, :, cols]
        send(line, line, agc_s.at[it, s, ch, 1], agc_r.at[it, s, ch, 1], sibling)

    def halves(it, s, ch):
        cols = pl.ds(ch * width, width)
        arrived(ag.at[it, s, :, x, 1 - c, :, cols], agc_s.at[it, s, ch, 0], agc_r.at[it, s, ch, 0], sibling)
        arrived(ag.at[it, s, :, 1 - x, 1 - c, :, cols], agc_s.at[it, s, ch, 1], agc_r.at[it, s, ch, 1], sibling)
        if not ready[0]:
            ready[0] = True
            loads[3].wait()
        gathered = ag[it, s, :, :, :, :, cols].reshape(nocc, width)
        product = jnp.dot(occ_v[...].reshape(local_aux * nocc, nocc), gathered, preferred_element_type=F32)
        for p in range(local_aux):
            half[s, :, pl.ds(p * nvir + ch * width, width)] = product[p * nocc : (p + 1) * nocc].astype(BF16)

    def exchange(it, s, ch):
        cols = pl.ds(ch * width, width)
        if not ready[1]:
            ready[1] = True
            for load in loads[4:]:
                load.wait()
        product = lax.dot_general(
            half[s], vir_v[cols, :], (((1,), (1,)), ((), ())), preferred_element_type=F32
        )
        ex[it, s, :, :, :, :, cols] = product.reshape(nz, 2, 2, rows, width)
        send(
            ex.at[it, s, :, :, 1 - c, :, cols], cr.at[it, s, :, :, :, cols],
            rc_s.at[it, s, ch], rc_r.at[it, s, ch], sibling,
        )

    def rs_x(it, s, ch):
        cols = pl.ds(ch * width, width)
        arrived(cr.at[it, s, :, :, :, cols], rc_s.at[it, s, ch], rc_r.at[it, s, ch], sibling)
        xs[it, s, :, :, cols] = (
            ex[it, s, :, 1 - x, c, :, cols] + cr[it, s, :, 1 - x, :, cols]
        ).astype(BF16)
        send(
            xs.at[it, s, :, :, cols], xr.at[it, s, :, :, cols],
            rx_s.at[it, s, ch], rx_r.at[it, s, ch], across,
        )
        xo[s, :, :, cols] = ex[it, s, :, x, c, :, cols] + cr[it, s, :, x, :, cols]

    def rs_z(it, s, ch):
        cols = pl.ds(ch * width, width)
        arrived(xr.at[it, s, :, :, cols], rx_s.at[it, s, ch], rx_r.at[it, s, ch], across)
        for k in near_first[::-1]:
            zs[it, s, k, :, cols] = (xo[s, up(k), :, cols] + xr[it, s, up(k), :, cols].astype(F32)).astype(BF16)
            send(
                zs.at[it, s, k, :, cols], zr.at[it, s, k, :, cols],
                rz_s.at[it, s, ch, k], rz_r.at[it, s, ch, k], dev(up(k), x, c),
            )
        zo[s, :, cols] = xo[s, z, :, cols] + xr[it, s, z, :, cols].astype(F32)

    def update(it, s, ch):
        cols = pl.ds(ch * width, width)
        total = zo[s, :, cols]
        for k in near_first:
            arrived(zr.at[it, s, k, :, cols], rz_s.at[it, s, ch, k], rz_r.at[it, s, ch, k], dev(down(k), x, c))
            total = total + zr[it, s, k, :, cols].astype(F32)
        new = 0.4 * resp[s, :, cols] + 0.6 * (right[s, :, cols] - total) / denom[:, cols]
        if it == ITERS - 1:
            out[:, s, cols] = new
        else:
            resp[s, :, cols] = new
            ag_start(it + 1, s, ch)

    ready = [False, False]
    steps = dict(
        ag_start=ag_start, ag_z=ag_z, ag_x=ag_x, halves=halves,
        exchange=exchange, rs_x=rs_x, rs_z=rs_z, update=update,
    )
    for name, it, s, ch in plan(states):
        steps[name](it, s, ch)
    for copy in sent:
        copy.wait_send()


def plan(states):
    units = states * CHUNKS
    link, core, hop, near = 10500 // units // 2, 1800 // units, 1000, 700
    took = dict(
        ag_start=150, ag_z=200, ag_x=100, halves=1100 // units,
        exchange=4400 // units, rs_x=200, rs_z=200, update=250,
    )
    free, order, now = dict(x=0, z=0, c=0), [], 0

    def carry(lane, begin, length, latency):
        free[lane] = max(free[lane], begin) + length
        return free[lane] + latency

    todo = [("ag_start", 0, s, ch) for s in range(states) for ch in range(CHUNKS)]
    for it in range(ITERS):
        for name in ("ag_z", "ag_x", "halves", "exchange", "rs_x", "rs_z", "update"):
            todo += [(name, it, s, ch) for s in range(states) for ch in range(CHUNKS)]
    arrival = {}
    done = set()
    while todo:

        def rank(step):
            name, it, s, ch = step
            if name == "exchange":
                needs = [("halves", it, s, each) in done for each in range(CHUNKS)]
                begin = 0 if all(needs) else 1 << 40
            else:
                begin = 0 if name == "ag_start" else arrival.get(step, 1 << 40)
            return (max(now, begin), name in ("halves", "exchange"), s, it, ch)

        step = min(todo, key=rank)
        name, it, s, ch = step
        now = max(now, rank(step)[0]) + took[name]
        todo.remove(step)
        done.add(step)
        order.append(step)
        if name == "ag_start" or (name == "update" and it + 1 < ITERS):
            ahead = it + (name == "update")
            arrival[("ag_z", ahead, s, ch)] = carry("z", now, link, hop)
            carry("x", now, link // 4, hop)
        elif name == "ag_z":
            arrival[("ag_x", it, s, ch)] = carry("x", now, link * 3 // 4, hop)
        elif name == "ag_x":
            arrival[("halves", it, s, ch)] = carry("c", now, core // 4, near)
        elif name == "exchange":
            arrival[("rs_x", it, s, ch)] = carry("c", now, core, near)
        elif name == "rs_x":
            arrival[("rs_z", it, s, ch)] = carry("x", now, link, hop)
        elif name == "rs_z":
            arrival[("update", it, s, ch)] = carry("z", now, link, hop)
    return order


def fused(rhs, occ_energy, vir_energy, occ_ints, vir_ints, devices):
    rows, states, nvir = rhs.shape
    local_aux, nocc, _ = occ_ints.shape
    nz = devices // 4
    dma = pltpu.SemaphoreType.DMA
    vmem = pl.BlockSpec(memory_space=pltpu.VMEM)
    hbm = pl.BlockSpec(memory_space=pltpu.HBM)
    lead = (ITERS, states)
    pair = lambda *shape: [dma(lead + shape)] * 2
    flops = ITERS * 2 * local_aux * nocc * states * nvir * (nocc + nvir)
    return pl.pallas_call(
        functools.partial(kernel, nz),
        out_shape=jax.ShapeDtypeStruct(rhs.shape, F32),
        in_specs=[hbm] * 5,
        out_specs=vmem,
        scratch_shapes=[
            pltpu.VMEM(rhs.shape, F32),
            pltpu.VMEM((1, nocc), F32),
            pltpu.VMEM((1, nvir), F32),
            pltpu.VMEM(occ_ints.shape, BF16),
            pltpu.VMEM((nvir, local_aux * nvir), BF16),
            pltpu.VMEM((rows, nvir), F32),
            pltpu.VMEM((states, rows, nvir), F32),
            pltpu.VMEM((states, rows, nvir), F32),
            pltpu.VMEM(lead + (nz, 2, 2, rows, nvir), BF16),
            pltpu.VMEM((states, nocc, local_aux * nvir), BF16),
            pltpu.VMEM(lead + (nz, 2, 2, rows, nvir), F32),
            pltpu.VMEM(lead + (nz, 2, rows, nvir), F32),
            pltpu.VMEM((states, nz, rows, nvir), F32),
            pltpu.VMEM(lead + (nz, rows, nvir), BF16),
            pltpu.VMEM(lead + (nz, rows, nvir), BF16),
            pltpu.VMEM((states, rows, nvir), F32),
            pltpu.VMEM(lead + (nz, rows, nvir), BF16),
            pltpu.VMEM(lead + (nz, rows, nvir), BF16),
            dma((local_aux + 4,)),
            *pair(CHUNKS, nz), *pair(CHUNKS, nz), *pair(CHUNKS, 2),
            *pair(CHUNKS), *pair(CHUNKS), *pair(CHUNKS, nz),
        ],
        compiler_params=pltpu.CompilerParams(
            collective_id=0, has_side_effects=True, vmem_limit_bytes=62 * 2**20
        ),
        cost_estimate=pl.CostEstimate(flops=flops, bytes_accessed=2 * vir_ints.size, transcendentals=0),
    )(rhs, occ_energy.reshape(1, nocc), vir_energy.reshape(1, nvir), occ_ints, vir_ints)


def collective(rhs, occ_energy, vir_energy, occ_ints, vir_ints):
    own_rows, states, nvir = rhs.shape
    local_aux, nocc, _ = occ_ints.shape
    position = lax.axis_index("aux")
    my_occ = lax.dynamic_slice_in_dim(occ_energy, position * own_rows, own_rows, 0)
    denom = vir_energy[None, None, :] - my_occ[:, None, None]
    response = rhs / denom
    for step in range(ITERS):
        rounded = response.astype(BF16)
        piece = lax.all_gather(rounded, "aux", axis=0, tiled=True)
        flat = piece.reshape(piece.shape[0], states * nvir)
        half = jnp.einsum("pij,jk->pik", occ_ints, flat, preferred_element_type=F32)
        half = half.astype(BF16).reshape(local_aux, nocc, states, nvir)
        exchange = lax.psum_scatter(
            lax.dot_general(half, vir_ints, (((0, 3), (0, 2)), ((), ())), preferred_element_type=F32),
            "aux", scatter_dimension=0, tiled=True,
        )
        response = 0.4 * response + 0.6 * (rhs - exchange) / denom
    return response


def solution(mesh):
    devices = mesh.shape["aux"]

    def shards(rhs, occ_energy, vir_energy, occ_ints, vir_ints):
        rows, states, nvir = rhs.shape
        if rows % 16 == 0 and devices % 4 == 0 and devices > 4 and states == 2:
            return fused(rhs, occ_energy, vir_energy, occ_ints, vir_ints, devices)
        return collective(rhs, occ_energy, vir_energy, occ_ints, vir_ints)

    split = P(("grp", "aux"), None, None)
    return jax.shard_map(
        shards, mesh=mesh, in_specs=(split, P("grp"), P("grp"), split, split), out_specs=split, check_vma=False
    )
```

```python
import functools

import jax
import jax.numpy as jnp
from jax import lax
from jax.experimental import pallas as pl
from jax.experimental.pallas import tpu as pltpu
from jax.sharding import PartitionSpec as P

ITERS = 2
CHUNKS = 2
MESH = pl.DeviceIdType.MESH
F32 = jnp.float32
BF16 = jnp.bfloat16


def kernel(
    nz, rhs_hbm, occ_e_hbm, vir_e_hbm, occ_hbm, vir_hbm, out,
    rhs, occ_e, vir_e, occ_v, vir_v, denom, right, resp, ag, half, ex, cr, xo, xs, xr, zo, zs, zr,
    load_sem, agz_s, agz_r, agx_s, agx_r, agc_s, agc_r,
    rc_s, rc_r, rx_s, rx_r, rz_s, rz_r,
):
    rows, states, nvir = rhs.shape
    nocc = half.shape[2]
    local_aux = occ_v.shape[0]
    width = nvir // CHUNKS
    grp = lax.axis_index("grp")
    me = lax.axis_index("aux")
    c = lax.rem(me, 2)
    x = lax.rem(me // 2, 2)
    z = me // 4

    def dev(zz, xx, cc):
        return (grp, (zz * 2 + xx) * 2 + cc)

    def up(k):
        return lax.rem(z + k, nz)

    def down(k):
        return lax.rem(z + nz - k, nz)

    sibling = dev(z, x, 1 - c)
    across = dev(z, 1 - x, c)

    pairs = [(rhs_hbm, rhs), (occ_e_hbm, occ_e), (vir_e_hbm, vir_e), (occ_hbm, occ_v)]
    pairs += [(vir_hbm.at[p], vir_v.at[:, pl.ds(p * nvir, nvir)]) for p in range(local_aux)]
    loads = [pltpu.make_async_copy(src, dst, load_sem.at[i]) for i, (src, dst) in enumerate(pairs)]
    for load in loads:
        load.start()

    barrier = pltpu.get_barrier_semaphore()
    for peer in [sibling, across] + [dev(up(k), x, c) for k in range(1, nz)]:
        pl.semaphore_signal(barrier, inc=1, device_id=peer, device_id_type=MESH)

    for load in loads[:3]:
        load.wait()
    picked = lax.broadcasted_iota(jnp.int32, (rows, nocc), 1) == (
        lax.broadcasted_iota(jnp.int32, (rows, nocc), 0) + me * rows
    )
    own_occ = jnp.sum(jnp.where(picked, occ_e[...], 0.0), axis=1, keepdims=True)
    denom[...] = vir_e[...] - own_occ
    for s in range(states):
        right[s] = rhs[:, s, :]
        resp[s] = right[s] / denom[...]
    pl.semaphore_wait(barrier, nz + 1)

    sent = []

    def send(src, dst, s_sem, r_sem, to):
        copy = pltpu.make_async_remote_copy(
            src_ref=src, dst_ref=dst, send_sem=s_sem, recv_sem=r_sem, device_id=to, device_id_type=MESH
        )
        copy.start()
        sent.append(copy)

    def arrived(dst, s_sem, r_sem, frm):
        pltpu.make_async_remote_copy(
            src_ref=dst, dst_ref=dst, send_sem=s_sem, recv_sem=r_sem, device_id=frm, device_id_type=MESH
        ).wait_recv()

    near_first = sorted(range(1, nz), key=lambda k: min(k, nz - k))

    def ag_start(it, s, ch):
        cols = pl.ds(ch * width, width)
        block = ag.at[it, s, z, x, c, :, cols]
        block[...] = resp[s, :, cols].astype(BF16)
        for k in near_first[::-1]:
            send(block, block, agz_s.at[it, s, ch, k], agz_r.at[it, s, ch, k], dev(up(k), x, c))
        send(block, block, agx_s.at[it, s, ch, 0], agx_r.at[it, s, ch, 0], across)

    def ag_z(it, s, ch):
        cols = pl.ds(ch * width, width)
        for k in near_first:
            block = ag.at[it, s, down(k), x, c, :, cols]
            arrived(block, agz_s.at[it, s, ch, k], agz_r.at[it, s, ch, k], dev(down(k), x, c))
            send(block, block, agx_s.at[it, s, ch, k], agx_r.at[it, s, ch, k], across)
        line = ag.at[it, s, :, x, c, :, cols]
        send(line, line, agc_s.at[it, s, ch, 0], agc_r.at[it, s, ch, 0], sibling)

    def ag_x(it, s, ch):
        cols = pl.ds(ch * width, width)
        for k in [0] + near_first:
            block = ag.at[it, s, down(k), 1 - x, c, :, cols]
            arrived(block, agx_s.at[it, s, ch, k], agx_r.at[it, s, ch, k], across)
        line = ag.at[it, s, :, 1 - x, c, :, cols]
        send(line, line, agc_s.at[it, s, ch, 1], agc_r.at[it, s, ch, 1], sibling)

    def halves(it, s, ch):
        cols = pl.ds(ch * width, width)
        arrived(ag.at[it, s, :, x, 1 - c, :, cols], agc_s.at[it, s, ch, 0], agc_r.at[it, s, ch, 0], sibling)
        arrived(ag.at[it, s, :, 1 - x, 1 - c, :, cols], agc_s.at[it, s, ch, 1], agc_r.at[it, s, ch, 1], sibling)
        if not ready[0]:
            ready[0] = True
            loads[3].wait()
        gathered = ag[it, s, :, :, :, :, cols].reshape(nocc, width)
        turned = gathered.T
        for p in range(local_aux):
            product = lax.dot_general(
                turned, occ_v[p], (((1,), (1,)), ((), ())), preferred_element_type=F32
            )
            half[s, pl.ds(p * nvir + ch * width, width), :] = product.astype(BF16)

    def exchange(it, s, ch):
        cols = pl.ds(ch * width, width)
        if not ready[1]:
            ready[1] = True
            for load in loads[4:]:
                load.wait()
        product = jnp.dot(vir_v[cols, :], half[s], preferred_element_type=F32)
        ex[it, s, :, :, :, :, cols] = product.T.reshape(nz, 2, 2, rows, width)
        send(
            ex.at[it, s, :, :, 1 - c, :, cols], cr.at[it, s, :, :, :, cols],
            rc_s.at[it, s, ch], rc_r.at[it, s, ch], sibling,
        )

    def rs_x(it, s, ch):
        cols = pl.ds(ch * width, width)
        arrived(cr.at[it, s, :, :, :, cols], rc_s.at[it, s, ch], rc_r.at[it, s, ch], sibling)
        xs[it, s, :, :, cols] = (
            ex[it, s, :, 1 - x, c, :, cols] + cr[it, s, :, 1 - x, :, cols]
        ).astype(BF16)
        send(
            xs.at[it, s, :, :, cols], xr.at[it, s, :, :, cols],
            rx_s.at[it, s, ch], rx_r.at[it, s, ch], across,
        )
        xo[s, :, :, cols] = ex[it, s, :, x, c, :, cols] + cr[it, s, :, x, :, cols]

    def rs_z(it, s, ch):
        cols = pl.ds(ch * width, width)
        arrived(xr.at[it, s, :, :, cols], rx_s.at[it, s, ch], rx_r.at[it, s, ch], across)
        for k in near_first[::-1]:
            zs[it, s, k, :, cols] = (xo[s, up(k), :, cols] + xr[it, s, up(k), :, cols].astype(F32)).astype(BF16)
            send(
                zs.at[it, s, k, :, cols], zr.at[it, s, k, :, cols],
                rz_s.at[it, s, ch, k], rz_r.at[it, s, ch, k], dev(up(k), x, c),
            )
        zo[s, :, cols] = xo[s, z, :, cols] + xr[it, s, z, :, cols].astype(F32)

    def update(it, s, ch):
        cols = pl.ds(ch * width, width)
        total = zo[s, :, cols]
        for k in near_first:
            arrived(zr.at[it, s, k, :, cols], rz_s.at[it, s, ch, k], rz_r.at[it, s, ch, k], dev(down(k), x, c))
            total = total + zr[it, s, k, :, cols].astype(F32)
        new = 0.4 * resp[s, :, cols] + 0.6 * (right[s, :, cols] - total) / denom[:, cols]
        if it == ITERS - 1:
            out[:, s, cols] = new
        else:
            resp[s, :, cols] = new
            ag_start(it + 1, s, ch)

    ready = [False, False]
    steps = dict(
        ag_start=ag_start, ag_z=ag_z, ag_x=ag_x, halves=halves,
        exchange=exchange, rs_x=rs_x, rs_z=rs_z, update=update,
    )
    for name, it, s, ch in plan(states):
        steps[name](it, s, ch)
    for copy in sent:
        copy.wait_send()


def plan(states):
    units = states * CHUNKS
    link, core, hop, near = 10500 // units // 2, 1800 // units, 1000, 700
    took = dict(
        ag_start=150, ag_z=200, ag_x=100, halves=1100 // units,
        exchange=4400 // units, rs_x=200, rs_z=200, update=250,
    )
    free, order, now = dict(x=0, z=0, c=0), [], 0

    def carry(lane, begin, length, latency):
        free[lane] = max(free[lane], begin) + length
        return free[lane] + latency

    todo = [("ag_start", 0, s, ch) for s in range(states) for ch in range(CHUNKS)]
    for it in range(ITERS):
        for name in ("ag_z", "ag_x", "halves", "exchange", "rs_x", "rs_z", "update"):
            todo += [(name, it, s, ch) for s in range(states) for ch in range(CHUNKS)]
    arrival = {}
    done = set()
    while todo:

        def rank(step):
            name, it, s, ch = step
            if name == "exchange":
                needs = [("halves", it, s, each) in done for each in range(CHUNKS)]
                begin = 0 if all(needs) else 1 << 40
            else:
                begin = 0 if name == "ag_start" else arrival.get(step, 1 << 40)
            return (max(now, begin), name in ("halves", "exchange"), s, it, ch)

        step = min(todo, key=rank)
        name, it, s, ch = step
        now = max(now, rank(step)[0]) + took[name]
        todo.remove(step)
        done.add(step)
        order.append(step)
        if name == "ag_start" or (name == "update" and it + 1 < ITERS):
            ahead = it + (name == "update")
            arrival[("ag_z", ahead, s, ch)] = carry("z", now, link, hop)
            carry("x", now, link // 4, hop)
        elif name == "ag_z":
            arrival[("ag_x", it, s, ch)] = carry("x", now, link * 3 // 4, hop)
        elif name == "ag_x":
            arrival[("halves", it, s, ch)] = carry("c", now, core // 4, near)
        elif name == "exchange":
            arrival[("rs_x", it, s, ch)] = carry("c", now, core, near)
        elif name == "rs_x":
            arrival[("rs_z", it, s, ch)] = carry("x", now, link, hop)
        elif name == "rs_z":
            arrival[("update", it, s, ch)] = carry("z", now, link, hop)
    return order


def fused(rhs, occ_energy, vir_energy, occ_ints, vir_ints, devices):
    rows, states, nvir = rhs.shape
    local_aux, nocc, _ = occ_ints.shape
    nz = devices // 4
    dma = pltpu.SemaphoreType.DMA
    vmem = pl.BlockSpec(memory_space=pltpu.VMEM)
    hbm = pl.BlockSpec(memory_space=pltpu.HBM)
    lead = (ITERS, states)
    pair = lambda *shape: [dma(lead + shape)] * 2
    flops = ITERS * 2 * local_aux * nocc * states * nvir * (nocc + nvir)
    return pl.pallas_call(
        functools.partial(kernel, nz),
        out_shape=jax.ShapeDtypeStruct(rhs.shape, F32),
        in_specs=[hbm] * 5,
        out_specs=vmem,
        scratch_shapes=[
            pltpu.VMEM(rhs.shape, F32),
            pltpu.VMEM((1, nocc), F32),
            pltpu.VMEM((1, nvir), F32),
            pltpu.VMEM(occ_ints.shape, BF16),
            pltpu.VMEM((nvir, local_aux * nvir), BF16),
            pltpu.VMEM((rows, nvir), F32),
            pltpu.VMEM((states, rows, nvir), F32),
            pltpu.VMEM((states, rows, nvir), F32),
            pltpu.VMEM(lead + (nz, 2, 2, rows, nvir), BF16),
            pltpu.VMEM((states, local_aux * nvir, nocc), BF16),
            pltpu.VMEM(lead + (nz, 2, 2, rows, nvir), F32),
            pltpu.VMEM(lead + (nz, 2, rows, nvir), F32),
            pltpu.VMEM((states, nz, rows, nvir), F32),
            pltpu.VMEM(lead + (nz, rows, nvir), BF16),
            pltpu.VMEM(lead + (nz, rows, nvir), BF16),
            pltpu.VMEM((states, rows, nvir), F32),
            pltpu.VMEM(lead + (nz, rows, nvir), BF16),
            pltpu.VMEM(lead + (nz, rows, nvir), BF16),
            dma((local_aux + 4,)),
            *pair(CHUNKS, nz), *pair(CHUNKS, nz), *pair(CHUNKS, 2),
            *pair(CHUNKS), *pair(CHUNKS), *pair(CHUNKS, nz),
        ],
        compiler_params=pltpu.CompilerParams(
            collective_id=0, has_side_effects=True, vmem_limit_bytes=62 * 2**20
        ),
        cost_estimate=pl.CostEstimate(flops=flops, bytes_accessed=2 * vir_ints.size, transcendentals=0),
    )(rhs, occ_energy.reshape(1, nocc), vir_energy.reshape(1, nvir), occ_ints, vir_ints)


def collective(rhs, occ_energy, vir_energy, occ_ints, vir_ints):
    own_rows, states, nvir = rhs.shape
    local_aux, nocc, _ = occ_ints.shape
    position = lax.axis_index("aux")
    my_occ = lax.dynamic_slice_in_dim(occ_energy, position * own_rows, own_rows, 0)
    denom = vir_energy[None, None, :] - my_occ[:, None, None]
    response = rhs / denom
    for step in range(ITERS):
        rounded = response.astype(BF16)
        piece = lax.all_gather(rounded, "aux", axis=0, tiled=True)
        flat = piece.reshape(piece.shape[0], states * nvir)
        half = jnp.einsum("pij,jk->pik", occ_ints, flat, preferred_element_type=F32)
        half = half.astype(BF16).reshape(local_aux, nocc, states, nvir)
        exchange = lax.psum_scatter(
            lax.dot_general(half, vir_ints, (((0, 3), (0, 2)), ((), ())), preferred_element_type=F32),
            "aux", scatter_dimension=0, tiled=True,
        )
        response = 0.4 * response + 0.6 * (rhs - exchange) / denom
    return response


def solution(mesh):
    devices = mesh.shape["aux"]

    def shards(rhs, occ_energy, vir_energy, occ_ints, vir_ints):
        rows, states, nvir = rhs.shape
        if rows % 16 == 0 and devices % 4 == 0 and devices > 4 and states == 2:
            return fused(rhs, occ_energy, vir_energy, occ_ints, vir_ints, devices)
        return collective(rhs, occ_energy, vir_energy, occ_ints, vir_ints)

    split = P(("grp", "aux"), None, None)
    return jax.shard_map(
        shards, mesh=mesh, in_specs=(split, P("grp"), P("grp"), split, split), out_specs=split, check_vma=False
    )
```

```python
import functools

import jax
import jax.numpy as jnp
from jax import lax
from jax.experimental import pallas as pl
from jax.experimental.pallas import tpu as pltpu
from jax.sharding import PartitionSpec as P

ITERS = 2
CHUNKS = 2
MESH = pl.DeviceIdType.MESH
F32 = jnp.float32
BF16 = jnp.bfloat16


def kernel(
    nz, rhs_hbm, occ_e_hbm, vir_e_hbm, occ_hbm, vir_hbm, out,
    rhs, occ_e, vir_e, occ_v, vir_v, denom, right, resp, ag, half, ex, cr, xo, xs, xr, zo, zs, zr,
    load_sem, agz_s, agz_r, agx_s, agx_r, agc_s, agc_r,
    rc_s, rc_r, rx_s, rx_r, rz_s, rz_r,
):
    rows, states, nvir = rhs.shape
    nocc = half.shape[1]
    local_aux = occ_v.shape[0]
    width = nvir // CHUNKS
    grp = lax.axis_index("grp")
    me = lax.axis_index("aux")
    c = lax.rem(me, 2)
    x = lax.rem(me // 2, 2)
    z = me // 4

    def dev(zz, xx, cc):
        return (grp, (zz * 2 + xx) * 2 + cc)

    def up(k):
        return lax.rem(z + k, nz)

    def down(k):
        return lax.rem(z + nz - k, nz)

    sibling = dev(z, x, 1 - c)
    across = dev(z, 1 - x, c)

    pairs = [(rhs_hbm, rhs), (occ_e_hbm, occ_e), (vir_e_hbm, vir_e), (occ_hbm, occ_v)]
    pairs += [(vir_hbm.at[p], vir_v.at[:, pl.ds(p * nvir, nvir)]) for p in range(local_aux)]
    loads = [pltpu.make_async_copy(src, dst, load_sem.at[i]) for i, (src, dst) in enumerate(pairs)]
    for load in loads:
        load.start()

    barrier = pltpu.get_barrier_semaphore()
    for peer in [sibling, across] + [dev(up(k), x, c) for k in range(1, nz)]:
        pl.semaphore_signal(barrier, inc=1, device_id=peer, device_id_type=MESH)

    for load in loads[:3]:
        load.wait()
    picked = lax.broadcasted_iota(jnp.int32, (rows, nocc), 1) == (
        lax.broadcasted_iota(jnp.int32, (rows, nocc), 0) + me * rows
    )
    own_occ = jnp.sum(jnp.where(picked, occ_e[...], 0.0), axis=1, keepdims=True)
    denom[...] = vir_e[...] - own_occ
    for s in range(states):
        right[s] = rhs[:, s, :]
        resp[s] = right[s] / denom[...]
    pl.semaphore_wait(barrier, nz + 1)

    sent = []

    def send(src, dst, s_sem, r_sem, to):
        copy = pltpu.make_async_remote_copy(
            src_ref=src, dst_ref=dst, send_sem=s_sem, recv_sem=r_sem, device_id=to, device_id_type=MESH
        )
        copy.start()
        sent.append(copy)

    def arrived(dst, s_sem, r_sem, frm):
        pltpu.make_async_remote_copy(
            src_ref=dst, dst_ref=dst, send_sem=s_sem, recv_sem=r_sem, device_id=frm, device_id_type=MESH
        ).wait_recv()

    near_first = sorted(range(1, nz), key=lambda k: min(k, nz - k))

    def ag_start(it, s, ch):
        cols = pl.ds(ch * width, width)
        block = ag.at[it, s, z, x, c, :, cols]
        block[...] = resp[s, :, cols].astype(BF16)
        for k in near_first[::-1]:
            send(block, block, agz_s.at[it, s, ch, k], agz_r.at[it, s, ch, k], dev(up(k), x, c))

    def ag_z(it, s, ch):
        cols = pl.ds(ch * width, width)
        for k in near_first:
            block = ag.at[it, s, down(k), x, c, :, cols]
            arrived(block, agz_s.at[it, s, ch, k], agz_r.at[it, s, ch, k], dev(down(k), x, c))
        line = ag.at[it, s, :, x, c, :, cols]
        send(line, line, agx_s.at[it, s, ch], agx_r.at[it, s, ch], across)
        send(line, line, agc_s.at[it, s, ch, 0], agc_r.at[it, s, ch, 0], sibling)

    def ag_x(it, s, ch):
        cols = pl.ds(ch * width, width)
        line = ag.at[it, s, :, 1 - x, c, :, cols]
        arrived(line, agx_s.at[it, s, ch], agx_r.at[it, s, ch], across)
        send(line, line, agc_s.at[it, s, ch, 1], agc_r.at[it, s, ch, 1], sibling)

    def halves(it, s, ch):
        cols = pl.ds(ch * width, width)
        arrived(ag.at[it, s, :, x, 1 - c, :, cols], agc_s.at[it, s, ch, 0], agc_r.at[it, s, ch, 0], sibling)
        arrived(ag.at[it, s, :, 1 - x, 1 - c, :, cols], agc_s.at[it, s, ch, 1], agc_r.at[it, s, ch, 1], sibling)
        if not ready[0]:
            ready[0] = True
            loads[3].wait()
        gathered = ag[it, s, :, :, :, :, cols].reshape(nocc, width)
        product = jnp.dot(occ_v[...].reshape(local_aux * nocc, nocc), gathered, preferred_element_type=F32)
        for p in range(local_aux):
            half[s, :, pl.ds(p * nvir + ch * width, width)] = product[p * nocc : (p + 1) * nocc].astype(BF16)

    def exchange(it, s, ch):
        cols = pl.ds(ch * width, width)
        if not ready[1]:
            ready[1] = True
            for load in loads[4:]:
                load.wait()
        product = lax.dot_general(
            half[s], vir_v[cols, :], (((1,), (1,)), ((), ())), preferred_element_type=F32
        )
        ex[it, s, :, :, :, :, cols] = product.reshape(nz, 2, 2, rows, width)
        send(
            ex.at[it, s, :, :, 1 - c, :, cols], cr.at[it, s, :, :, :, cols],
            rc_s.at[it, s, ch], rc_r.at[it, s, ch], sibling,
        )

    def rs_x(it, s, ch):
        cols = pl.ds(ch * width, width)
        arrived(cr.at[it, s, :, :, :, cols], rc_s.at[it, s, ch], rc_r.at[it, s, ch], sibling)
        xs[it, s, :, :, cols] = (
            ex[it, s, :, 1 - x, c, :, cols] + cr[it, s, :, 1 - x, :, cols]
        ).astype(BF16)
        send(
            xs.at[it, s, :, :, cols], xr.at[it, s, :, :, cols],
            rx_s.at[it, s, ch], rx_r.at[it, s, ch], across,
        )
        xo[s, :, :, cols] = ex[it, s, :, x, c, :, cols] + cr[it, s, :, x, :, cols]

    def rs_z(it, s, ch):
        cols = pl.ds(ch * width, width)
        arrived(xr.at[it, s, :, :, cols], rx_s.at[it, s, ch], rx_r.at[it, s, ch], across)
        for k in near_first[::-1]:
            zs[it, s, k, :, cols] = (xo[s, up(k), :, cols] + xr[it, s, up(k), :, cols].astype(F32)).astype(BF16)
            send(
                zs.at[it, s, k, :, cols], zr.at[it, s, k, :, cols],
                rz_s.at[it, s, ch, k], rz_r.at[it, s, ch, k], dev(up(k), x, c),
            )
        zo[s, :, cols] = xo[s, z, :, cols] + xr[it, s, z, :, cols].astype(F32)

    def update(it, s, ch):
        cols = pl.ds(ch * width, width)
        total = zo[s, :, cols]
        for k in near_first:
            arrived(zr.at[it, s, k, :, cols], rz_s.at[it, s, ch, k], rz_r.at[it, s, ch, k], dev(down(k), x, c))
            total = total + zr[it, s, k, :, cols].astype(F32)
        new = 0.4 * resp[s, :, cols] + 0.6 * (right[s, :, cols] - total) / denom[:, cols]
        if it == ITERS - 1:
            out[:, s, cols] = new
        else:
            resp[s, :, cols] = new
            ag_start(it + 1, s, ch)

    ready = [False, False]
    retired = 0
    steps = dict(
        ag_start=ag_start, ag_z=ag_z, ag_x=ag_x, halves=halves,
        exchange=exchange, rs_x=rs_x, rs_z=rs_z, update=update,
    )
    order = plan(states)
    begun = []
    for at, (name, it, s, ch) in enumerate(order):
        begun.append(len(sent))
        if at >= len(order) - 8:
            while retired < begun[at - 8]:
                sent[retired].wait_send()
                retired += 1
        steps[name](it, s, ch)
    for copy in sent[retired:]:
        copy.wait_send()


def plan(states):
    units = states * CHUNKS
    link, core, hop, near = 10500 // units // 2, 1800 // units, 1500, 1000
    took = dict(
        ag_start=500, ag_z=400, ag_x=200, halves=1600 // units,
        exchange=7000 // units, rs_x=300, rs_z=500, update=700,
    )
    free, order, now = dict(x=0, z=0, c=0), [], 0

    def carry(lane, begin, length, latency):
        free[lane] = max(free[lane], begin) + length
        return free[lane] + latency

    todo = [("ag_start", 0, s, ch) for s in range(states) for ch in range(CHUNKS)]
    for it in range(ITERS):
        for name in ("ag_z", "ag_x", "halves", "exchange", "rs_x", "rs_z", "update"):
            todo += [(name, it, s, ch) for s in range(states) for ch in range(CHUNKS)]
    arrival = {}
    done = set()
    while todo:

        def rank(step):
            name, it, s, ch = step
            if name == "exchange":
                needs = [("halves", it, s, each) in done for each in range(CHUNKS)]
                begin = 0 if all(needs) else 1 << 40
            else:
                begin = 0 if name == "ag_start" else arrival.get(step, 1 << 40)
            return (max(now, begin), name in ("halves", "exchange"), s, it, ch)

        step = min(todo, key=rank)
        name, it, s, ch = step
        now = max(now, rank(step)[0]) + took[name]
        todo.remove(step)
        done.add(step)
        order.append(step)
        if name == "ag_start" or (name == "update" and it + 1 < ITERS):
            ahead = it + (name == "update")
            arrival[("ag_z", ahead, s, ch)] = carry("z", now, link, hop)
        elif name == "ag_z":
            arrival[("ag_x", it, s, ch)] = carry("x", now, link, hop)
        elif name == "ag_x":
            arrival[("halves", it, s, ch)] = carry("c", now, core // 4, near)
        elif name == "exchange":
            arrival[("rs_x", it, s, ch)] = carry("c", now, core, near)
        elif name == "rs_x":
            arrival[("rs_z", it, s, ch)] = carry("x", now, link, hop)
        elif name == "rs_z":
            arrival[("update", it, s, ch)] = carry("z", now, link, hop)
    return order


def fused(rhs, occ_energy, vir_energy, occ_ints, vir_ints, devices):
    rows, states, nvir = rhs.shape
    local_aux, nocc, _ = occ_ints.shape
    nz = devices // 4
    dma = pltpu.SemaphoreType.DMA
    vmem = pl.BlockSpec(memory_space=pltpu.VMEM)
    hbm = pl.BlockSpec(memory_space=pltpu.HBM)
    lead = (ITERS, states)
    pair = lambda *shape: [dma(lead + shape)] * 2
    flops = ITERS * 2 * local_aux * nocc * states * nvir * (nocc + nvir)
    return pl.pallas_call(
        functools.partial(kernel, nz),
        out_shape=jax.ShapeDtypeStruct(rhs.shape, F32),
        in_specs=[hbm] * 5,
        out_specs=vmem,
        scratch_shapes=[
            pltpu.VMEM(rhs.shape, F32),
            pltpu.VMEM((1, nocc), F32),
            pltpu.VMEM((1, nvir), F32),
            pltpu.VMEM(occ_ints.shape, BF16),
            pltpu.VMEM((nvir, local_aux * nvir), BF16),
            pltpu.VMEM((rows, nvir), F32),
            pltpu.VMEM((states, rows, nvir), F32),
            pltpu.VMEM((states, rows, nvir), F32),
            pltpu.VMEM(lead + (nz, 2, 2, rows, nvir), BF16),
            pltpu.VMEM((states, nocc, local_aux * nvir), BF16),
            pltpu.VMEM(lead + (nz, 2, 2, rows, nvir), F32),
            pltpu.VMEM(lead + (nz, 2, rows, nvir), F32),
            pltpu.VMEM((states, nz, rows, nvir), F32),
            pltpu.VMEM(lead + (nz, rows, nvir), BF16),
            pltpu.VMEM(lead + (nz, rows, nvir), BF16),
            pltpu.VMEM((states, rows, nvir), F32),
            pltpu.VMEM(lead + (nz, rows, nvir), BF16),
            pltpu.VMEM(lead + (nz, rows, nvir), BF16),
            dma((local_aux + 4,)),
            *pair(CHUNKS, nz), *pair(CHUNKS), *pair(CHUNKS, 2),
            *pair(CHUNKS), *pair(CHUNKS), *pair(CHUNKS, nz),
        ],
        compiler_params=pltpu.CompilerParams(
            collective_id=0, has_side_effects=True, vmem_limit_bytes=62 * 2**20
        ),
        cost_estimate=pl.CostEstimate(flops=flops, bytes_accessed=2 * vir_ints.size, transcendentals=0),
    )(rhs, occ_energy.reshape(1, nocc), vir_energy.reshape(1, nvir), occ_ints, vir_ints)


def collective(rhs, occ_energy, vir_energy, occ_ints, vir_ints):
    own_rows, states, nvir = rhs.shape
    local_aux, nocc, _ = occ_ints.shape
    position = lax.axis_index("aux")
    my_occ = lax.dynamic_slice_in_dim(occ_energy, position * own_rows, own_rows, 0)
    denom = vir_energy[None, None, :] - my_occ[:, None, None]
    response = rhs / denom
    for step in range(ITERS):
        rounded = response.astype(BF16)
        piece = lax.all_gather(rounded, "aux", axis=0, tiled=True)
        flat = piece.reshape(piece.shape[0], states * nvir)
        half = jnp.einsum("pij,jk->pik", occ_ints, flat, preferred_element_type=F32)
        half = half.astype(BF16).reshape(local_aux, nocc, states, nvir)
        exchange = lax.psum_scatter(
            lax.dot_general(half, vir_ints, (((0, 3), (0, 2)), ((), ())), preferred_element_type=F32),
            "aux", scatter_dimension=0, tiled=True,
        )
        response = 0.4 * response + 0.6 * (rhs - exchange) / denom
    return response


def solution(mesh):
    devices = mesh.shape["aux"]

    def shards(rhs, occ_energy, vir_energy, occ_ints, vir_ints):
        rows, states, nvir = rhs.shape
        if rows % 16 == 0 and devices % 4 == 0 and devices > 4 and states == 2:
            return fused(rhs, occ_energy, vir_energy, occ_ints, vir_ints, devices)
        return collective(rhs, occ_energy, vir_energy, occ_ints, vir_ints)

    split = P(("grp", "aux"), None, None)
    return jax.shard_map(
        shards, mesh=mesh, in_specs=(split, P("grp"), P("grp"), split, split), out_specs=split, check_vma=False
    )
```

```python
import functools

import jax
import jax.numpy as jnp
from jax import lax
from jax.experimental import pallas as pl
from jax.experimental.pallas import tpu as pltpu
from jax.sharding import PartitionSpec as P

ITERS = 2
CHUNKS = 2
MESH = pl.DeviceIdType.MESH
F32 = jnp.float32
BF16 = jnp.bfloat16


def kernel(
    nz, rhs_hbm, occ_e_hbm, vir_e_hbm, occ_hbm, vir_hbm, out,
    rhs, occ_e, vir_e, occ_v, vir_v, denom, right, resp, ag, half, ex, cr, xo, xs, xr, zo, zs, zr,
    load_sem, agz_s, agz_r, agx_s, agx_r, agc_s, agc_r,
    rc_s, rc_r, rx_s, rx_r, rz_s, rz_r,
):
    rows, states, nvir = rhs.shape
    nocc = half.shape[1]
    local_aux = occ_v.shape[0]
    width = nvir // CHUNKS
    grp = lax.axis_index("grp")
    me = lax.axis_index("aux")
    c = lax.rem(me, 2)
    x = lax.rem(me // 2, 2)
    z = me // 4

    def dev(zz, xx, cc):
        return (grp, (zz * 2 + xx) * 2 + cc)

    def up(k):
        return lax.rem(z + k, nz)

    def down(k):
        return lax.rem(z + nz - k, nz)

    sibling = dev(z, x, 1 - c)
    across = dev(z, 1 - x, c)

    pairs = [(rhs_hbm, rhs), (occ_e_hbm, occ_e), (vir_e_hbm, vir_e), (occ_hbm, occ_v)]
    pairs += [(vir_hbm.at[p], vir_v.at[:, pl.ds(p * nvir, nvir)]) for p in range(local_aux)]
    loads = [pltpu.make_async_copy(src, dst, load_sem.at[i]) for i, (src, dst) in enumerate(pairs)]
    for load in loads:
        load.start()

    barrier = pltpu.get_barrier_semaphore()
    for peer in [sibling, across] + [dev(up(k), x, c) for k in range(1, nz)]:
        pl.semaphore_signal(barrier, inc=1, device_id=peer, device_id_type=MESH)

    for load in loads[:3]:
        load.wait()
    picked = lax.broadcasted_iota(jnp.int32, (rows, nocc), 1) == (
        lax.broadcasted_iota(jnp.int32, (rows, nocc), 0) + me * rows
    )
    own_occ = jnp.sum(jnp.where(picked, occ_e[...], 0.0), axis=1, keepdims=True)
    denom[...] = vir_e[...] - own_occ
    for s in range(states):
        right[s] = rhs[:, s, :]
        resp[s] = right[s] / denom[...]
    pl.semaphore_wait(barrier, nz + 1)

    sent = []

    def send(src, dst, s_sem, r_sem, to):
        copy = pltpu.make_async_remote_copy(
            src_ref=src, dst_ref=dst, send_sem=s_sem, recv_sem=r_sem, device_id=to, device_id_type=MESH
        )
        copy.start()
        sent.append(copy)

    def arrived(dst, s_sem, r_sem, frm):
        pltpu.make_async_remote_copy(
            src_ref=dst, dst_ref=dst, send_sem=s_sem, recv_sem=r_sem, device_id=frm, device_id_type=MESH
        ).wait_recv()

    near_first = sorted(range(1, nz), key=lambda k: min(k, nz - k))

    def ag_start(it, s, ch):
        cols = pl.ds(ch * width, width)
        block = ag.at[it, s, z, x, c, :, cols]
        block[...] = resp[s, :, cols].astype(BF16)
        for k in near_first[::-1]:
            send(block, block, agz_s.at[it, s, ch, k], agz_r.at[it, s, ch, k], dev(up(k), x, c))

    def ag_z(it, s, ch):
        cols = pl.ds(ch * width, width)
        for k in near_first:
            block = ag.at[it, s, down(k), x, c, :, cols]
            arrived(block, agz_s.at[it, s, ch, k], agz_r.at[it, s, ch, k], dev(down(k), x, c))
        line = ag.at[it, s, :, x, c, :, cols]
        send(line, line, agx_s.at[it, s, ch], agx_r.at[it, s, ch], across)
        send(line, line, agc_s.at[it, s, ch, 0], agc_r.at[it, s, ch, 0], sibling)

    def ag_x(it, s, ch):
        cols = pl.ds(ch * width, width)
        line = ag.at[it, s, :, 1 - x, c, :, cols]
        arrived(line, agx_s.at[it, s, ch], agx_r.at[it, s, ch], across)
        send(line, line, agc_s.at[it, s, ch, 1], agc_r.at[it, s, ch, 1], sibling)

    def halves(it, s, ch):
        cols = pl.ds(ch * width, width)
        arrived(ag.at[it, s, :, x, 1 - c, :, cols], agc_s.at[it, s, ch, 0], agc_r.at[it, s, ch, 0], sibling)
        arrived(ag.at[it, s, :, 1 - x, 1 - c, :, cols], agc_s.at[it, s, ch, 1], agc_r.at[it, s, ch, 1], sibling)
        if not ready[0]:
            ready[0] = True
            loads[3].wait()
        gathered = ag[it, s, :, :, :, :, cols].reshape(nocc, width)
        product = jnp.dot(occ_v[...].reshape(local_aux * nocc, nocc), gathered, preferred_element_type=F32)
        for p in range(local_aux):
            half[s, :, pl.ds(p * nvir + ch * width, width)] = product[p * nocc : (p + 1) * nocc].astype(BF16)

    def exchange(it, _, ch):
        cols = pl.ds(ch * width, width)
        if not ready[1]:
            ready[1] = True
            for load in loads[4:]:
                load.wait()
        product = lax.dot_general(
            half[...].reshape(states * nocc, local_aux * nvir), vir_v[cols, :], (((1,), (1,)), ((), ())), preferred_element_type=F32
        )
        for s in range(states):
            part = product[s * nocc : (s + 1) * nocc]
            ex[it, s, :, :, :, :, cols] = part.reshape(nz, 2, 2, rows, width)
            send(
                ex.at[it, s, :, :, 1 - c, :, cols], cr.at[it, s, :, :, :, cols],
                rc_s.at[it, s, ch], rc_r.at[it, s, ch], sibling,
            )

    def rs_x(it, s, ch):
        cols = pl.ds(ch * width, width)
        arrived(cr.at[it, s, :, :, :, cols], rc_s.at[it, s, ch], rc_r.at[it, s, ch], sibling)
        xs[it, s, :, :, cols] = (
            ex[it, s, :, 1 - x, c, :, cols] + cr[it, s, :, 1 - x, :, cols]
        ).astype(BF16)
        send(
            xs.at[it, s, :, :, cols], xr.at[it, s, :, :, cols],
            rx_s.at[it, s, ch], rx_r.at[it, s, ch], across,
        )
        xo[s, :, :, cols] = ex[it, s, :, x, c, :, cols] + cr[it, s, :, x, :, cols]

    def rs_z(it, s, ch):
        cols = pl.ds(ch * width, width)
        arrived(xr.at[it, s, :, :, cols], rx_s.at[it, s, ch], rx_r.at[it, s, ch], across)
        for k in near_first[::-1]:
            zs[it, s, k, :, cols] = (xo[s, up(k), :, cols] + xr[it, s, up(k), :, cols].astype(F32)).astype(BF16)
            send(
                zs.at[it, s, k, :, cols], zr.at[it, s, k, :, cols],
                rz_s.at[it, s, ch, k], rz_r.at[it, s, ch, k], dev(up(k), x, c),
            )
        zo[s, :, cols] = xo[s, z, :, cols] + xr[it, s, z, :, cols].astype(F32)

    def update(it, s, ch):
        cols = pl.ds(ch * width, width)
        total = zo[s, :, cols]
        for k in near_first:
            arrived(zr.at[it, s, k, :, cols], rz_s.at[it, s, ch, k], rz_r.at[it, s, ch, k], dev(down(k), x, c))
            total = total + zr[it, s, k, :, cols].astype(F32)
        new = 0.4 * resp[s, :, cols] + 0.6 * (right[s, :, cols] - total) / denom[:, cols]
        if it == ITERS - 1:
            out[:, s, cols] = new
        else:
            resp[s, :, cols] = new
            ag_start(it + 1, s, ch)

    ready = [False, False]
    retired = 0
    steps = dict(
        ag_start=ag_start, ag_z=ag_z, ag_x=ag_x, halves=halves,
        exchange=exchange, rs_x=rs_x, rs_z=rs_z, update=update,
    )
    order = plan(states)
    begun = []
    for at, (name, it, s, ch) in enumerate(order):
        begun.append(len(sent))
        if at >= len(order) - 8:
            while retired < begun[at - 8]:
                sent[retired].wait_send()
                retired += 1
        steps[name](it, s, ch)
    for copy in sent[retired:]:
        copy.wait_send()


def plan(states):
    units = states * CHUNKS
    link, core, hop, near = 10500 // units // 2, 1800 // units, 1500, 1000
    took = dict(
        ag_start=500, ag_z=400, ag_x=200, halves=1600 // units,
        exchange=5000 // CHUNKS, rs_x=300, rs_z=500, update=700,
    )
    free, order, now = dict(x=0, z=0, c=0), [], 0

    def carry(lane, begin, length, latency):
        free[lane] = max(free[lane], begin) + length
        return free[lane] + latency

    todo = [("ag_start", 0, s, ch) for s in range(states) for ch in range(CHUNKS)]
    for it in range(ITERS):
        for name in ("ag_z", "ag_x", "halves", "exchange", "rs_x", "rs_z", "update"):
            own = range(1 if name == "exchange" else states)
            todo += [(name, it, s, ch) for s in own for ch in range(CHUNKS)]
    arrival = {}
    done = set()
    while todo:

        def rank(step):
            name, it, s, ch = step
            if name == "exchange":
                needs = [("halves", it, t, each) in done for t in range(states) for each in range(CHUNKS)]
                begin = 0 if all(needs) else 1 << 40
            else:
                begin = 0 if name == "ag_start" else arrival.get(step, 1 << 40)
            return (max(now, begin), name in ("halves", "exchange"), s, it, ch)

        step = min(todo, key=rank)
        name, it, s, ch = step
        now = max(now, rank(step)[0]) + took[name]
        todo.remove(step)
        done.add(step)
        order.append(step)
        if name == "ag_start" or (name == "update" and it + 1 < ITERS):
            ahead = it + (name == "update")
            arrival[("ag_z", ahead, s, ch)] = carry("z", now, link, hop)
        elif name == "ag_z":
            arrival[("ag_x", it, s, ch)] = carry("x", now, link, hop)
        elif name == "ag_x":
            arrival[("halves", it, s, ch)] = carry("c", now, core // 4, near)
        elif name == "exchange":
            for t in range(states):
                arrival[("rs_x", it, t, ch)] = carry("c", now, core, near)
        elif name == "rs_x":
            arrival[("rs_z", it, s, ch)] = carry("x", now, link, hop)
        elif name == "rs_z":
            arrival[("update", it, s, ch)] = carry("z", now, link, hop)
    return order


def fused(rhs, occ_energy, vir_energy, occ_ints, vir_ints, devices):
    rows, states, nvir = rhs.shape
    local_aux, nocc, _ = occ_ints.shape
    nz = devices // 4
    dma = pltpu.SemaphoreType.DMA
    vmem = pl.BlockSpec(memory_space=pltpu.VMEM)
    hbm = pl.BlockSpec(memory_space=pltpu.HBM)
    lead = (ITERS, states)
    pair = lambda *shape: [dma(lead + shape)] * 2
    flops = ITERS * 2 * local_aux * nocc * states * nvir * (nocc + nvir)
    return pl.pallas_call(
        functools.partial(kernel, nz),
        out_shape=jax.ShapeDtypeStruct(rhs.shape, F32),
        in_specs=[hbm] * 5,
        out_specs=vmem,
        scratch_shapes=[
            pltpu.VMEM(rhs.shape, F32),
            pltpu.VMEM((1, nocc), F32),
            pltpu.VMEM((1, nvir), F32),
            pltpu.VMEM(occ_ints.shape, BF16),
            pltpu.VMEM((nvir, local_aux * nvir), BF16),
            pltpu.VMEM((rows, nvir), F32),
            pltpu.VMEM((states, rows, nvir), F32),
            pltpu.VMEM((states, rows, nvir), F32),
            pltpu.VMEM(lead + (nz, 2, 2, rows, nvir), BF16),
            pltpu.VMEM((states, nocc, local_aux * nvir), BF16),
            pltpu.VMEM(lead + (nz, 2, 2, rows, nvir), F32),
            pltpu.VMEM(lead + (nz, 2, rows, nvir), F32),
            pltpu.VMEM((states, nz, rows, nvir), F32),
            pltpu.VMEM(lead + (nz, rows, nvir), BF16),
            pltpu.VMEM(lead + (nz, rows, nvir), BF16),
            pltpu.VMEM((states, rows, nvir), F32),
            pltpu.VMEM(lead + (nz, rows, nvir), BF16),
            pltpu.VMEM(lead + (nz, rows, nvir), BF16),
            dma((local_aux + 4,)),
            *pair(CHUNKS, nz), *pair(CHUNKS), *pair(CHUNKS, 2),
            *pair(CHUNKS), *pair(CHUNKS), *pair(CHUNKS, nz),
        ],
        compiler_params=pltpu.CompilerParams(
            collective_id=0, has_side_effects=True, vmem_limit_bytes=62 * 2**20
        ),
        cost_estimate=pl.CostEstimate(flops=flops, bytes_accessed=2 * vir_ints.size, transcendentals=0),
    )(rhs, occ_energy.reshape(1, nocc), vir_energy.reshape(1, nvir), occ_ints, vir_ints)


def collective(rhs, occ_energy, vir_energy, occ_ints, vir_ints):
    own_rows, states, nvir = rhs.shape
    local_aux, nocc, _ = occ_ints.shape
    position = lax.axis_index("aux")
    my_occ = lax.dynamic_slice_in_dim(occ_energy, position * own_rows, own_rows, 0)
    denom = vir_energy[None, None, :] - my_occ[:, None, None]
    response = rhs / denom
    for step in range(ITERS):
        rounded = response.astype(BF16)
        piece = lax.all_gather(rounded, "aux", axis=0, tiled=True)
        flat = piece.reshape(piece.shape[0], states * nvir)
        half = jnp.einsum("pij,jk->pik", occ_ints, flat, preferred_element_type=F32)
        half = half.astype(BF16).reshape(local_aux, nocc, states, nvir)
        exchange = lax.psum_scatter(
            lax.dot_general(half, vir_ints, (((0, 3), (0, 2)), ((), ())), preferred_element_type=F32),
            "aux", scatter_dimension=0, tiled=True,
        )
        response = 0.4 * response + 0.6 * (rhs - exchange) / denom
    return response


def solution(mesh):
    devices = mesh.shape["aux"]

    def shards(rhs, occ_energy, vir_energy, occ_ints, vir_ints):
        rows, states, nvir = rhs.shape
        if rows % 16 == 0 and devices % 4 == 0 and devices > 4 and states == 2:
            return fused(rhs, occ_energy, vir_energy, occ_ints, vir_ints, devices)
        return collective(rhs, occ_energy, vir_energy, occ_ints, vir_ints)

    split = P(("grp", "aux"), None, None)
    return jax.shard_map(
        shards, mesh=mesh, in_specs=(split, P("grp"), P("grp"), split, split), out_specs=split, check_vma=False
    )
```

```python
import functools

import jax
import jax.numpy as jnp
from jax import lax
from jax.experimental import pallas as pl
from jax.experimental.pallas import tpu as pltpu
from jax.sharding import PartitionSpec as P

ITERS = 2
CHUNKS = 2
MESH = pl.DeviceIdType.MESH
F32 = jnp.float32
BF16 = jnp.bfloat16


def kernel(
    nz, rhs_hbm, occ_e_hbm, vir_e_hbm, occ_hbm, vir_hbm, out,
    rhs, occ_e, vir_e, occ_v, vir_v, denom, right, resp, ag, half, ex, cr, xo, xs, xr, zo, zs, zr,
    load_sem, agz_s, agz_r, agx_s, agx_r, agc_s, agc_r,
    rc_s, rc_r, rx_s, rx_r, rz_s, rz_r,
):
    rows, states, nvir = rhs.shape
    nocc = half.shape[1]
    local_aux = occ_v.shape[0]
    width = nvir // CHUNKS
    grp = lax.axis_index("grp")
    me = lax.axis_index("aux")
    c = lax.rem(me, 2)
    x = lax.rem(me // 2, 2)
    z = me // 4

    def dev(zz, xx, cc):
        return (grp, (zz * 2 + xx) * 2 + cc)

    def up(k):
        return lax.rem(z + k, nz)

    def down(k):
        return lax.rem(z + nz - k, nz)

    sibling = dev(z, x, 1 - c)
    across = dev(z, 1 - x, c)

    pairs = [(rhs_hbm, rhs), (occ_e_hbm, occ_e), (vir_e_hbm, vir_e), (occ_hbm, occ_v)]
    pairs += [(vir_hbm.at[p], vir_v.at[:, pl.ds(p * nvir, nvir)]) for p in range(local_aux)]
    loads = [pltpu.make_async_copy(src, dst, load_sem.at[i]) for i, (src, dst) in enumerate(pairs)]
    for load in loads:
        load.start()

    barrier = pltpu.get_barrier_semaphore()
    for peer in [sibling, across] + [dev(up(k), x, c) for k in range(1, nz)]:
        pl.semaphore_signal(barrier, inc=1, device_id=peer, device_id_type=MESH)

    for load in loads[:3]:
        load.wait()
    picked = lax.broadcasted_iota(jnp.int32, (rows, nocc), 1) == (
        lax.broadcasted_iota(jnp.int32, (rows, nocc), 0) + me * rows
    )
    own_occ = jnp.sum(jnp.where(picked, occ_e[...], 0.0), axis=1, keepdims=True)
    denom[...] = vir_e[...] - own_occ
    for s in range(states):
        right[s] = rhs[:, s, :]
        resp[s] = right[s] / denom[...]
    pl.semaphore_wait(barrier, nz + 1)

    sent = []

    def send(src, dst, s_sem, r_sem, to):
        copy = pltpu.make_async_remote_copy(
            src_ref=src, dst_ref=dst, send_sem=s_sem, recv_sem=r_sem, device_id=to, device_id_type=MESH
        )
        copy.start()
        sent.append(copy)

    def arrived(dst, s_sem, r_sem, frm):
        pltpu.make_async_remote_copy(
            src_ref=dst, dst_ref=dst, send_sem=s_sem, recv_sem=r_sem, device_id=frm, device_id_type=MESH
        ).wait_recv()

    near_first = sorted(range(1, nz), key=lambda k: min(k, nz - k))

    def ag_start(it, s, ch):
        cols = pl.ds(ch * width, width)
        block = ag.at[it, s, z, x, c, :, cols]
        block[...] = resp[s, :, cols].astype(BF16)
        for k in near_first[::-1]:
            send(block, block, agz_s.at[it, s, ch, k], agz_r.at[it, s, ch, k], dev(up(k), x, c))

    def ag_z(it, s, ch):
        cols = pl.ds(ch * width, width)
        for k in near_first:
            block = ag.at[it, s, down(k), x, c, :, cols]
            arrived(block, agz_s.at[it, s, ch, k], agz_r.at[it, s, ch, k], dev(down(k), x, c))
        line = ag.at[it, s, :, x, c, :, cols]
        send(line, line, agx_s.at[it, s, ch], agx_r.at[it, s, ch], across)
        send(line, line, agc_s.at[it, s, ch, 0], agc_r.at[it, s, ch, 0], sibling)

    def ag_x(it, s, ch):
        cols = pl.ds(ch * width, width)
        line = ag.at[it, s, :, 1 - x, c, :, cols]
        arrived(line, agx_s.at[it, s, ch], agx_r.at[it, s, ch], across)
        send(line, line, agc_s.at[it, s, ch, 1], agc_r.at[it, s, ch, 1], sibling)

    def halves(it, s, ch):
        cols = pl.ds(ch * width, width)
        arrived(ag.at[it, s, :, x, 1 - c, :, cols], agc_s.at[it, s, ch, 0], agc_r.at[it, s, ch, 0], sibling)
        arrived(ag.at[it, s, :, 1 - x, 1 - c, :, cols], agc_s.at[it, s, ch, 1], agc_r.at[it, s, ch, 1], sibling)
        if not ready[0]:
            ready[0] = True
            loads[3].wait()
        gathered = ag[it, s, :, :, :, :, cols].reshape(nocc, width)
        product = jnp.dot(occ_v[...].reshape(local_aux * nocc, nocc), gathered, preferred_element_type=F32)
        for p in range(local_aux):
            half[s, :, pl.ds(p * nvir + ch * width, width)] = product[p * nocc : (p + 1) * nocc].astype(BF16)

    def exchange(it, s, ch):
        cols = pl.ds(ch * width, width)
        if not ready[1]:
            ready[1] = True
            for load in loads[4:]:
                load.wait()
        product = lax.dot_general(
            half[s], vir_v[cols, :], (((1,), (1,)), ((), ())), preferred_element_type=F32
        )
        ex[it, s, :, :, :, :, cols] = product.reshape(nz, 2, 2, rows, width)
        send(
            ex.at[it, s, :, :, 1 - c, :, cols], cr.at[it, s, :, :, :, cols],
            rc_s.at[it, s, ch], rc_r.at[it, s, ch], sibling,
        )

    def rs_x(it, s, ch):
        cols = pl.ds(ch * width, width)
        arrived(cr.at[it, s, :, :, :, cols], rc_s.at[it, s, ch], rc_r.at[it, s, ch], sibling)
        xs[it, s, :, :, cols] = (
            ex[it, s, :, 1 - x, c, :, cols] + cr[it, s, :, 1 - x, :, cols]
        ).astype(BF16)
        send(
            xs.at[it, s, :, :, cols], xr.at[it, s, :, :, cols],
            rx_s.at[it, s, ch], rx_r.at[it, s, ch], across,
        )
        xo[s, :, :, cols] = ex[it, s, :, x, c, :, cols] + cr[it, s, :, x, :, cols]

    def rs_z(it, s, ch):
        cols = pl.ds(ch * width, width)
        arrived(xr.at[it, s, :, :, cols], rx_s.at[it, s, ch], rx_r.at[it, s, ch], across)
        for k in near_first[::-1]:
            zs[it, s, k, :, cols] = (xo[s, up(k), :, cols] + xr[it, s, up(k), :, cols].astype(F32)).astype(BF16)
            send(
                zs.at[it, s, k, :, cols], zr.at[it, s, k, :, cols],
                rz_s.at[it, s, ch, k], rz_r.at[it, s, ch, k], dev(up(k), x, c),
            )
        zo[s, :, cols] = xo[s, z, :, cols] + xr[it, s, z, :, cols].astype(F32)

    def update(it, s, ch):
        cols = pl.ds(ch * width, width)
        total = zo[s, :, cols]
        for k in near_first:
            arrived(zr.at[it, s, k, :, cols], rz_s.at[it, s, ch, k], rz_r.at[it, s, ch, k], dev(down(k), x, c))
            total = total + zr[it, s, k, :, cols].astype(F32)
        new = 0.4 * resp[s, :, cols] + 0.6 * (right[s, :, cols] - total) / denom[:, cols]
        if it == ITERS - 1:
            out[:, s, cols] = new
        else:
            resp[s, :, cols] = new
            ag_start(it + 1, s, ch)

    ready = [False, False]
    retired = 0
    steps = dict(
        ag_start=ag_start, ag_z=ag_z, ag_x=ag_x, halves=halves,
        exchange=exchange, rs_x=rs_x, rs_z=rs_z, update=update,
    )
    order = plan(states)
    begun = []
    for at, (name, it, s, ch) in enumerate(order):
        begun.append(len(sent))
        if at >= len(order) - 8:
            while retired < begun[at - 8]:
                sent[retired].wait_send()
                retired += 1
        steps[name](it, s, ch)
    for copy in sent[retired:]:
        copy.wait_send()


def plan(states):
    units = states * CHUNKS
    link, core, hop, near = 10500 // units // 2, 1800 // units, 1500, 1000
    took = dict(
        ag_start=500, ag_z=400, ag_x=200, halves=1600 // units,
        exchange=7000 // units, rs_x=300, rs_z=500, update=700,
    )
    free, order, now = dict(x=0, z=0, c=0), [], 0

    def carry(lane, begin, length, latency):
        free[lane] = max(free[lane], begin) + length
        return free[lane] + latency

    todo = [("ag_start", 0, s, ch) for s in range(states) for ch in range(CHUNKS)]
    for it in range(ITERS):
        for name in ("ag_z", "ag_x", "halves", "exchange", "rs_x", "rs_z", "update"):
            todo += [(name, it, s, ch) for s in range(states) for ch in range(CHUNKS)]
    arrival = {}
    done = set()
    while todo:

        def rank(step):
            name, it, s, ch = step
            if name == "exchange":
                needs = [("halves", it, s, each) in done for each in range(CHUNKS)]
                begin = 0 if all(needs) else 1 << 40
            else:
                begin = arrival.get(step, 1 << 40)
                if name == "ag_start":
                    begin = 0 if s == 0 or ("ag_z", 0, s - 1, 0) in done else 1 << 40
            return (max(now, begin), name in ("halves", "exchange"), s, it, ch)

        step = min(todo, key=rank)
        name, it, s, ch = step
        now = max(now, rank(step)[0]) + took[name]
        todo.remove(step)
        done.add(step)
        order.append(step)
        if name == "ag_start" or (name == "update" and it + 1 < ITERS):
            ahead = it + (name == "update")
            arrival[("ag_z", ahead, s, ch)] = carry("z", now, link, hop)
        elif name == "ag_z":
            arrival[("ag_x", it, s, ch)] = carry("x", now, link, hop)
        elif name == "ag_x":
            arrival[("halves", it, s, ch)] = carry("c", now, core // 4, near)
        elif name == "exchange":
            arrival[("rs_x", it, s, ch)] = carry("c", now, core, near)
        elif name == "rs_x":
            arrival[("rs_z", it, s, ch)] = carry("x", now, link, hop)
        elif name == "rs_z":
            arrival[("update", it, s, ch)] = carry("z", now, link, hop)
    return order


def fused(rhs, occ_energy, vir_energy, occ_ints, vir_ints, devices):
    rows, states, nvir = rhs.shape
    local_aux, nocc, _ = occ_ints.shape
    nz = devices // 4
    dma = pltpu.SemaphoreType.DMA
    vmem = pl.BlockSpec(memory_space=pltpu.VMEM)
    hbm = pl.BlockSpec(memory_space=pltpu.HBM)
    lead = (ITERS, states)
    pair = lambda *shape: [dma(lead + shape)] * 2
    flops = ITERS * 2 * local_aux * nocc * states * nvir * (nocc + nvir)
    return pl.pallas_call(
        functools.partial(kernel, nz),
        out_shape=jax.ShapeDtypeStruct(rhs.shape, F32),
        in_specs=[hbm] * 5,
        out_specs=vmem,
        scratch_shapes=[
            pltpu.VMEM(rhs.shape, F32),
            pltpu.VMEM((1, nocc), F32),
            pltpu.VMEM((1, nvir), F32),
            pltpu.VMEM(occ_ints.shape, BF16),
            pltpu.VMEM((nvir, local_aux * nvir), BF16),
            pltpu.VMEM((rows, nvir), F32),
            pltpu.VMEM((states, rows, nvir), F32),
            pltpu.VMEM((states, rows, nvir), F32),
            pltpu.VMEM(lead + (nz, 2, 2, rows, nvir), BF16),
            pltpu.VMEM((states, nocc, local_aux * nvir), BF16),
            pltpu.VMEM(lead + (nz, 2, 2, rows, nvir), F32),
            pltpu.VMEM(lead + (nz, 2, rows, nvir), F32),
            pltpu.VMEM((states, nz, rows, nvir), F32),
            pltpu.VMEM(lead + (nz, rows, nvir), BF16),
            pltpu.VMEM(lead + (nz, rows, nvir), BF16),
            pltpu.VMEM((states, rows, nvir), F32),
            pltpu.VMEM(lead + (nz, rows, nvir), BF16),
            pltpu.VMEM(lead + (nz, rows, nvir), BF16),
            dma((local_aux + 4,)),
            *pair(CHUNKS, nz), *pair(CHUNKS), *pair(CHUNKS, 2),
            *pair(CHUNKS), *pair(CHUNKS), *pair(CHUNKS, nz),
        ],
        compiler_params=pltpu.CompilerParams(
            collective_id=0, has_side_effects=True, vmem_limit_bytes=62 * 2**20
        ),
        cost_estimate=pl.CostEstimate(flops=flops, bytes_accessed=2 * vir_ints.size, transcendentals=0),
    )(rhs, occ_energy.reshape(1, nocc), vir_energy.reshape(1, nvir), occ_ints, vir_ints)


def collective(rhs, occ_energy, vir_energy, occ_ints, vir_ints):
    own_rows, states, nvir = rhs.shape
    local_aux, nocc, _ = occ_ints.shape
    position = lax.axis_index("aux")
    my_occ = lax.dynamic_slice_in_dim(occ_energy, position * own_rows, own_rows, 0)
    denom = vir_energy[None, None, :] - my_occ[:, None, None]
    response = rhs / denom
    for step in range(ITERS):
        rounded = response.astype(BF16)
        piece = lax.all_gather(rounded, "aux", axis=0, tiled=True)
        flat = piece.reshape(piece.shape[0], states * nvir)
        half = jnp.einsum("pij,jk->pik", occ_ints, flat, preferred_element_type=F32)
        half = half.astype(BF16).reshape(local_aux, nocc, states, nvir)
        exchange = lax.psum_scatter(
            lax.dot_general(half, vir_ints, (((0, 3), (0, 2)), ((), ())), preferred_element_type=F32),
            "aux", scatter_dimension=0, tiled=True,
        )
        response = 0.4 * response + 0.6 * (rhs - exchange) / denom
    return response


def solution(mesh):
    devices = mesh.shape["aux"]

    def shards(rhs, occ_energy, vir_energy, occ_ints, vir_ints):
        rows, states, nvir = rhs.shape
        if rows % 16 == 0 and devices % 4 == 0 and devices > 4 and states == 2:
            return fused(rhs, occ_energy, vir_energy, occ_ints, vir_ints, devices)
        return collective(rhs, occ_energy, vir_energy, occ_ints, vir_ints)

    split = P(("grp", "aux"), None, None)
    return jax.shard_map(
        shards, mesh=mesh, in_specs=(split, P("grp"), P("grp"), split, split), out_specs=split, check_vma=False
    )
```
